32 devices in a mesh: expert: 8 (over y, x, core), dp: 4 (over z).
Axes of the slice: x: 2, y: 2, z: 4, core: 2. Of those that a mesh axis runs over, the one named last changes fastest.
Arguments:
- tokens: bfloat16 [4096, 2048], P(('dp', 'expert')), parts along dimension 0, may hold values from -6 to 6
- expert_ids: int32 [4096, 4], P(('dp', 'expert')), parts along dimension 0, may hold values from 0 to 7, all different within a row; in each aligned block of 128 rows (0 to 127, 128 to 255, ...) at most 96 rows name the same one
- gate_weights: bfloat16 [4096, 4], P(('dp', 'expert')), parts along dimension 0, may hold values from 0.049804688 to 1
- w_gate: bfloat16 [8, 2048, 768], P('expert'), may hold values from -0.125 to 0.125
- w_up: bfloat16 [8, 2048, 768], P('expert'), may hold values from -0.125 to 0.125
- w_down: bfloat16 [8, 768, 2048], P('expert'), may hold values from -0.21875 to 0.21875
Outputs:
- mixed: bfloat16 [4096, 2048], P(('dp', 'expert')), parts along dimension 0
The draws below stay inside these ranges and needn't reach their ends.
There are 4 independent parts, one for each index of `dp`. The reference program is written for one: setup_inputs(seed, part) draws one part's arguments, and reference() takes and returns one part's arrays. A program takes and returns all parts, laid end to end along the dimension named above; an argument that names none is the same for every part. Nothing has to cross between parts.
Inputs may be any that keep to these rules, and one draw needn't show every extreme that they name: `expert_ids`: each row names 4 different experts. In each aligned block of 128 rows (the rows of one device) no expert is named by more than 96 rows, a bound that some block reaches.
All inputs are finite; a program needn't handle non-finite values.
Results may differ from the reference program's by a relative error of at most 0.0049.
Values may be sent and summed in bfloat16 or wider, within the bound.
No kernel may reach another device: no remote copies, remote signals or barrier semaphores. Data moves between devices by JAX's collectives and lax.ppermute only.
A program may use at most 128 MiB of HBM per device.

```python
import math
import jax
import jax.numpy as jnp
import numpy as np
from jax import lax

D = 2048
FF = 768
TOP = 4
TOK_DEV = 128
EXPERTS = 8
TOKENS = 1024
MOST = 96


def steps_of(stream_key, dims, split, least, largest):
    def one(dim, shards_of):
        steps = jax.random.uniform(jax.random.fold_in(jax.random.fold_in(stream_key, 6), dim), (shards_of,), jnp.float32, least / len(split), largest / len(split))
        return jnp.repeat(jnp.exp(steps), dims[dim] // shards_of).reshape((-1,) + (1,) * (len(dims) - dim - 1))

    loudness = one(*split[0])
    for cut in split[1:]:
        loudness = loudness * one(*cut)
    return loudness


def routed_block(stream_key, own, number, rows, number_of, top, limit, slope):
    order = jax.random.permutation(stream_key, number_of)
    packed, usual = portions_of(number_of, rows * top, limit, slope, True), portions_of(number_of, rows * top, limit, slope, False)
    places = jnp.arange(number_of)

    def named(lengths, turn):
        used = int((lengths > 0).sum())
        fixed = max(1, used // 4)
        passed = fixed + (places - fixed + turn * (used - fixed)) % max(1, number_of - fixed)
        return jnp.zeros((number_of,), jnp.int32).at[order[jnp.where(places < fixed, places, passed)]].set(jnp.asarray(lengths, jnp.int32))

    lengths = jnp.where(number % 4 == 0, named(packed, number // 4), named(usual, number - number // 4 - 1))
    mixed = jax.random.permutation(jax.random.fold_in(own, 3), number_of)
    donor, sink = mixed[0:number_of // 2 * 2:2], mixed[1:number_of // 2 * 2:2]
    margin = jnp.minimum(lengths[donor] - 1, limit - lengths[sink]) // 2
    margin = jnp.where((donor == order[0]) | (sink == order[0]) | (lengths[sink] == 0), 0, jnp.maximum(margin, 0))
    passed = jax.random.randint(jax.random.fold_in(own, 4), (number_of // 2,), 0, 1 << 20) % (margin + 1)
    lengths = lengths.at[donor].add(-passed).at[sink].add(passed)
    items = jnp.searchsorted(jnp.cumsum(lengths), jnp.arange(rows * top), side="right").astype(jnp.int32)
    grid = items.reshape(top, rows).T
    grid = grid[jax.random.permutation(jax.random.fold_in(own, 1), rows)]
    turn = jax.random.randint(jax.random.fold_in(own, 2), (rows, 1), 0, top)
    return jnp.take_along_axis(grid, (jnp.arange(top)[None, :] + turn) % top, axis=1)


def portions_of(count, total, most, skew, full):
    loads = [(1 << 20) // math.isqrt(standing ** skew) + 1 for standing in range(1, count + 1)]
    largest = most if full else min(most, max(-(-total // count), total * loads[0] // sum(loads)))
    least = 1 if total - largest >= count - 1 else 0
    given, rest = [largest] + [least] * (count - 1), total - largest - least * (count - 1)
    while rest > 0:
        free = [i for i in range(1, count) if given[i] < largest] or [i for i in range(1, count) if given[i] < most]
        mass, budget = sum([loads[i] for i in free]), rest
        for i in free:
            extra = min(most - given[i], max(1, budget * loads[i] // mass), rest)
            given[i] = given[i] + extra
            rest = rest - extra
    return np.array(given)


def gaussian(stream_key, extent, spread, limit, shards=(), held_as=jnp.bfloat16):
    result = spread * jax.random.normal(stream_key, extent, jnp.float32)
    if shards:
        result = result * steps_of(stream_key, extent, shards, -0.22, 0.18)
    return jnp.clip(result, -limit, limit).astype(held_as)


def setup_inputs(seed: int = 0, part: int = 0) -> dict:
    key_of = jax.random.split(jax.random.key(seed), 7)
    part_splits = jax.random.split(jax.random.fold_in(key_of[6], part), 7)
    tokens = gaussian(part_splits[0], (TOKENS, D), 1.0, 6.0, ((0, 8),))
    expert_ids_keys = jax.random.split(jax.random.fold_in(part_splits[1], 1), TOKENS // TOK_DEV)
    expert_ids_turns = jax.random.permutation(jax.random.fold_in(part_splits[1], 3), TOKENS // TOK_DEV)
    expert_ids = jax.vmap(lambda own, number: routed_block(jax.random.fold_in(part_splits[1], 2), own, number, TOK_DEV, EXPERTS, TOP, MOST, 1))(expert_ids_keys, expert_ids_turns).reshape((TOKENS, TOP))
    gate_weights = jnp.clip(0.049804688 + 0.9501953 * jax.random.uniform(part_splits[2], (TOKENS, TOP), jnp.float32) ** steps_of(part_splits[2], (TOKENS, TOP), ((0, 8),), -0.2, 0.2), 0.049804688, 1.0).astype(jnp.bfloat16)
    w_gate = gaussian(key_of[3], (EXPERTS, D, FF), D ** -0.5, 0.125, ((0, 8),))
    w_up = gaussian(key_of[4], (EXPERTS, D, FF), D ** -0.5, 0.125, ((0, 8),))
    w_down = gaussian(key_of[5], (EXPERTS, FF, D), FF ** -0.5, 0.21875, ((0, 8),))
    return {"tokens": tokens, "expert_ids": expert_ids, "gate_weights": gate_weights, "w_gate": w_gate, "w_up": w_up, "w_down": w_down}


def reference(tokens, expert_ids, gate_weights, w_gate, w_up, w_down):
    labels = jnp.arange(EXPERTS, dtype=jnp.int32)
    matched = expert_ids[:, :, None] == labels[None, None, :]
    route = jnp.sum(jnp.where(matched, gate_weights.astype(jnp.float32)[:, :, None], jnp.float32(0.0)), axis=1)

    def one_expert(combined, pieces):
        gate_part, up_part, down_part, column = pieces
        gate_act = jnp.dot(tokens, gate_part, preferred_element_type=jnp.float32)
        up_act = jnp.dot(tokens, up_part, preferred_element_type=jnp.float32)
        hidden = (jax.nn.silu(gate_act) * up_act).astype(jnp.bfloat16)
        expert_out = jnp.dot(hidden, down_part, preferred_element_type=jnp.float32)
        return combined + column[:, None] * expert_out, None

    start = jnp.zeros((tokens.shape[0], tokens.shape[1]), jnp.float32)
    combined, unused = lax.scan(one_expert, start, (w_gate, w_up, w_down, route.T))
    return combined.astype(jnp.bfloat16)
```

```python
import functools

import jax
import jax.numpy as jnp
from jax import lax
from jax.experimental import pallas as pl
from jax.experimental.pallas import tpu as pltpu
from jax.sharding import PartitionSpec as P

AXIS = "expert"
CORE, XBIT, YBIT = 1, 2, 4


def slot_table(routed, capacity):
    counted = routed.astype(jnp.int32)
    position = jnp.cumsum(counted, axis=1) - 1
    slot_ids = jnp.arange(capacity, dtype=jnp.int32)
    chosen = routed[:, None, :] & (position[:, None, :] == slot_ids[None, :, None])
    row_ids = jnp.arange(routed.shape[1], dtype=jnp.int32)
    slot_index = jnp.sum(jnp.where(chosen, row_ids[None, None, :], 0), axis=2)
    filled = jnp.any(chosen, axis=2)
    return (slot_index, filled)


def expert_ffn(slot_block, w_gate, w_up, w_down):
    width = slot_block.shape[-1]
    flat_rows = slot_block.reshape(-1, width)
    gate_act = jnp.dot(flat_rows, w_gate[0], preferred_element_type=jnp.float32)
    up_act = jnp.dot(flat_rows, w_up[0], preferred_element_type=jnp.float32)
    hidden = (jax.nn.silu(gate_act) * up_act).astype(jnp.bfloat16)
    expert_out = jnp.dot(hidden, w_down[0], preferred_element_type=jnp.float32)
    return expert_out.reshape(slot_block.shape[:-1] + (w_down.shape[2],))


def swap_all(rows):
    return lax.all_to_all(rows, AXIS, split_axis=0, concat_axis=0, tiled=True)


def route_table(expert_ids, gate_weights, experts):
    labels = jnp.arange(experts, dtype=jnp.int32)
    matched = expert_ids[:, :, None] == labels[None, None, :]
    weights = gate_weights.astype(jnp.float32)[:, :, None]
    return jnp.sum(jnp.where(matched, weights, jnp.float32(0.0)), axis=1)


def any_slice(tokens, expert_ids, gate_weights, w_gate, w_up, w_down):
    tok_dev, choose_k = expert_ids.shape
    width = tokens.shape[1]
    experts = w_gate.shape[0] * lax.axis_size(AXIS)
    capacity = min(tok_dev, 3 * tok_dev * choose_k // (2 * experts))
    weight = route_table(expert_ids, gate_weights, experts)
    home_index, home_filled = slot_table(weight.T != 0.0, capacity)
    arrived = swap_all(tokens[home_index])
    returned_rows = swap_all(expert_ffn(arrived, w_gate, w_up, w_down))
    owners = jnp.arange(experts, dtype=jnp.int32)[:, None]
    factor = jnp.where(home_filled, weight.T[owners, home_index], jnp.float32(0.0))
    combined = jnp.zeros((tok_dev, width), jnp.float32)
    combined = combined.at[home_index.reshape(-1)].add(
        (factor[:, :, None] * returned_rows).reshape(-1, width)
    )
    return combined.astype(jnp.bfloat16)


def hop(block, bits):
    return lax.ppermute(block, AXIS, [(i, i ^ bits) for i in range(lax.axis_size(AXIS))])


def ffn_body(pieces, *refs):
    n = len(pieces)
    x_refs = refs[:n]
    route_ref = refs[n]
    weights = refs[n + 1 : n + 7]
    o_refs = refs[n + 7 : 2 * n + 7]
    x_buf, *bufs, x_sem, w_sem = refs[2 * n + 7 :]
    starts = [sum(pieces[:k]) for k in range(n)]
    x_copies = [
        pltpu.make_async_copy(x_refs[k], x_buf.at[pl.ds(starts[k], pieces[k])], x_sem.at[k])
        for k in range(n)
    ]
    w_copies = [pltpu.make_async_copy(weights[k], bufs[k], w_sem.at[k]) for k in range(6)]
    w_copies[0].start()
    for copy in x_copies:
        copy.start()
    for copy in w_copies[1:]:
        copy.start()
    for copy in x_copies:
        copy.wait()
    x = x_buf[...]
    total = None
    for e in range(2):
        w_copies[3 * e].wait()
        gate = jnp.dot(x, bufs[3 * e][...], preferred_element_type=jnp.float32)
        w_copies[3 * e + 1].wait()
        up = jnp.dot(x, bufs[3 * e + 1][...], preferred_element_type=jnp.float32)
        hidden = (gate / (1.0 + jnp.exp(-gate)) * up).astype(jnp.bfloat16)
        w_copies[3 * e + 2].wait()
        out = jnp.dot(hidden, bufs[3 * e + 2][...], preferred_element_type=jnp.float32)
        out = route_ref[:, e : e + 1] * out
        total = out if total is None else total + out
    total = total.astype(jnp.bfloat16)
    for k in range(n):
        o_refs[k][...] = total[starts[k] : starts[k] + pieces[k]]


def ffn(blocks, route, weights):
    pieces = tuple(block.shape[0] for block in blocks)
    rows, width = sum(pieces), blocks[0].shape[1]
    hidden = weights[0].shape[1]
    moved = sum(w.size * 2 for w in weights) + 4 * rows * width
    return pl.pallas_call(
        functools.partial(ffn_body, pieces),
        out_shape=[jax.ShapeDtypeStruct((p, width), jnp.bfloat16) for p in pieces],
        in_specs=[pl.BlockSpec(memory_space=pl.ANY)] * len(blocks)
        + [pl.BlockSpec(memory_space=pltpu.VMEM)]
        + [pl.BlockSpec(memory_space=pl.ANY)] * 6,
        out_specs=[pl.BlockSpec(memory_space=pltpu.VMEM)] * len(blocks),
        scratch_shapes=[pltpu.VMEM((rows, width), jnp.bfloat16)]
        + [pltpu.VMEM(w.shape, jnp.bfloat16) for w in weights]
        + [pltpu.SemaphoreType.DMA((len(blocks),)), pltpu.SemaphoreType.DMA((6,))],
        compiler_params=pltpu.CompilerParams(vmem_limit_bytes=40 * 1024 * 1024),
        cost_estimate=pl.CostEstimate(
            flops=12 * rows * width * hidden, bytes_accessed=moved, transcendentals=2 * rows * hidden
        ),
    )(*blocks, route, *weights)


def two_by_two(tokens, expert_ids, gate_weights, w_gate, w_up, w_down):
    tok_dev = tokens.shape[0]
    half = tok_dev // 2
    me = lax.axis_index(AXIS)
    route = route_table(expert_ids, gate_weights, lax.axis_size(AXIS)).astype(jnp.bfloat16)
    routes = lax.all_gather(route, AXIS, axis=0)
    top, low = tokens[:half], tokens[half:]

    x_top, y_low = hop(top, XBIT), hop(low, YBIT)
    own = (w_gate[0], w_up[0], w_down[0])
    weights = own + tuple(hop(w, CORE) for w in own)
    d_top, d_low = hop(x_top, YBIT), hop(y_low, XBIT)
    x_low, y_top = hop(low, XBIT), hop(top, YBIT)

    def columns(bits, rows):
        table = lax.dynamic_index_in_dim(routes, me ^ bits, 0, keepdims=False)[rows]
        pair = [lax.dynamic_index_in_dim(table, me ^ b, 1) for b in (0, CORE)]
        return jnp.concatenate(pair, axis=1).astype(jnp.float32)

    tops, lows, both = slice(0, half), slice(half, tok_dev), slice(0, tok_dev)
    first = [columns(XBIT, tops), columns(YBIT, lows), columns(XBIT | YBIT, both)]
    second = [columns(0, both), columns(XBIT, lows), columns(YBIT, tops)]
    ox_top, oy_low, od_top, od_low = ffn(
        [x_top, y_low, d_top, d_low], jnp.concatenate(first), weights
    )
    e_top, e_low = hop(od_top, XBIT), hop(od_low, YBIT)
    fx_top, fy_low = hop(ox_top, XBIT), hop(oy_low, YBIT)
    o_own, ox_low, oy_top = ffn([tokens, x_low, y_top], jnp.concatenate(second), weights)
    f32 = lambda a: a.astype(jnp.float32)
    my_top = hop((f32(oy_top) + f32(e_top)).astype(jnp.bfloat16), YBIT)
    mx_low = hop((f32(ox_low) + f32(e_low)).astype(jnp.bfloat16), XBIT)
    out_top = f32(o_own[:half]) + f32(fx_top) + f32(my_top)
    out_low = f32(o_own[half:]) + f32(fy_low) + f32(mx_low)
    return jnp.concatenate([out_top, out_low]).astype(jnp.bfloat16)


def solution(mesh):
    return jax.shard_map(
        two_by_two if mesh.shape[AXIS] == 8 else any_slice,
        mesh=mesh,
        in_specs=(
            P(("dp", AXIS), None),
            P(("dp", AXIS), None),
            P(("dp", AXIS), None),
            P(AXIS, None, None),
            P(AXIS, None, None),
            P(AXIS, None, None),
        ),
        out_specs=P(("dp", AXIS), None),
        check_vma=False,
    )
```

```python
import functools

import jax
import jax.numpy as jnp
from jax import lax
from jax.experimental import pallas as pl
from jax.experimental.pallas import tpu as pltpu
from jax.sharding import PartitionSpec as P

AXIS = "expert"
CORE, XBIT, YBIT = 1, 2, 4


def slot_table(routed, capacity):
    counted = routed.astype(jnp.int32)
    position = jnp.cumsum(counted, axis=1) - 1
    slot_ids = jnp.arange(capacity, dtype=jnp.int32)
    chosen = routed[:, None, :] & (position[:, None, :] == slot_ids[None, :, None])
    row_ids = jnp.arange(routed.shape[1], dtype=jnp.int32)
    slot_index = jnp.sum(jnp.where(chosen, row_ids[None, None, :], 0), axis=2)
    filled = jnp.any(chosen, axis=2)
    return (slot_index, filled)


def expert_ffn(slot_block, w_gate, w_up, w_down):
    width = slot_block.shape[-1]
    flat_rows = slot_block.reshape(-1, width)
    gate_act = jnp.dot(flat_rows, w_gate[0], preferred_element_type=jnp.float32)
    up_act = jnp.dot(flat_rows, w_up[0], preferred_element_type=jnp.float32)
    hidden = (jax.nn.silu(gate_act) * up_act).astype(jnp.bfloat16)
    expert_out = jnp.dot(hidden, w_down[0], preferred_element_type=jnp.float32)
    return expert_out.reshape(slot_block.shape[:-1] + (w_down.shape[2],))


def swap_all(rows):
    return lax.all_to_all(rows, AXIS, split_axis=0, concat_axis=0, tiled=True)


def route_table(expert_ids, gate_weights, experts):
    labels = jnp.arange(experts, dtype=jnp.int32)
    matched = expert_ids[:, :, None] == labels[None, None, :]
    weights = gate_weights.astype(jnp.float32)[:, :, None]
    return jnp.sum(jnp.where(matched, weights, jnp.float32(0.0)), axis=1)


def any_slice(tokens, expert_ids, gate_weights, w_gate, w_up, w_down):
    tok_dev, choose_k = expert_ids.shape
    width = tokens.shape[1]
    experts = w_gate.shape[0] * lax.axis_size(AXIS)
    capacity = min(tok_dev, 3 * tok_dev * choose_k // (2 * experts))
    weight = route_table(expert_ids, gate_weights, experts)
    home_index, home_filled = slot_table(weight.T != 0.0, capacity)
    arrived = swap_all(tokens[home_index])
    returned_rows = swap_all(expert_ffn(arrived, w_gate, w_up, w_down))
    owners = jnp.arange(experts, dtype=jnp.int32)[:, None]
    factor = jnp.where(home_filled, weight.T[owners, home_index], jnp.float32(0.0))
    combined = jnp.zeros((tok_dev, width), jnp.float32)
    combined = combined.at[home_index.reshape(-1)].add(
        (factor[:, :, None] * returned_rows).reshape(-1, width)
    )
    return combined.astype(jnp.bfloat16)


def hop(block, bits):
    return lax.ppermute(block, AXIS, [(i, i ^ bits) for i in range(lax.axis_size(AXIS))])


def in_vmem(array):
    return pltpu.with_memory_space_constraint(array, pltpu.VMEM)


def vmem_out(shape):
    return pltpu.VMEM(shape, jnp.bfloat16)


MIB = 1 << 20
VMEM_SPEC = pl.BlockSpec(memory_space=pltpu.VMEM)
ANY_SPEC = pl.BlockSpec(memory_space=pl.ANY)


def label_body(tokens_ref, ids_ref, gates_ref, *refs):
    *out_refs, ids_buf, gates_buf, sem = refs
    width = tokens_ref.shape[1]
    rows, tail = ids_ref.shape[1], out_refs[0].shape[1] - width
    pairs = [(ids_ref, ids_buf), (gates_ref, gates_buf)]
    at = 0
    for out_ref in out_refs:
        part = out_ref.shape[0]
        pairs.append((tokens_ref.at[pl.ds(at, part)], out_ref.at[:, pl.ds(0, width)]))
        at += part
    copies = [pltpu.make_async_copy(src, dst, sem.at[k]) for k, (src, dst) in enumerate(pairs)]
    for copy in copies:
        copy.start()
    for copy in copies[:2]:
        copy.wait()
    me = lax.axis_index(AXIS)
    column = lax.broadcasted_iota(jnp.int32, (tail, rows), 0)
    gates = gates_buf[...].astype(jnp.float32)
    route = jnp.zeros((tail, rows), jnp.float32)
    for k in range(ids_ref.shape[0]):
        route += jnp.where(column == ids_buf[k : k + 1, :] ^ me, gates[k : k + 1, :], 0.0)
    route = route.T.astype(jnp.bfloat16)
    at = 0
    for out_ref in out_refs:
        part = out_ref.shape[0]
        out_ref[:, width:] = route[at : at + part]
        at += part
    for copy in copies[2:]:
        copy.wait()


def label(tokens, expert_ids, gate_weights, tail, parts):
    rows, width = tokens.shape
    arrays = (tokens, expert_ids.T, gate_weights.T)
    return pl.pallas_call(
        label_body,
        out_shape=[vmem_out((rows // parts, width + tail))] * parts,
        in_specs=[ANY_SPEC] * 3,
        out_specs=[VMEM_SPEC] * parts,
        scratch_shapes=[pltpu.VMEM(a.shape, a.dtype) for a in arrays[1:]]
        + [pltpu.SemaphoreType.DMA((2 + parts,))],
        compiler_params=pltpu.CompilerParams(vmem_limit_bytes=8 * MIB),
    )(*[pltpu.with_memory_space_constraint(a, pltpu.HBM) for a in arrays])


def after_body(n, *refs):
    for src, dst in zip(refs[:n], refs[-n:]):
        dst[...] = src[...]


def after(blocks, arrived):
    n = len(blocks)
    return pl.pallas_call(
        functools.partial(after_body, n),
        out_shape=[vmem_out(b.shape) for b in blocks],
        in_specs=[VMEM_SPEC] * n + [ANY_SPEC] * len(arrived),
        out_specs=[VMEM_SPEC] * n,
        compiler_params=pltpu.CompilerParams(vmem_limit_bytes=8 * MIB),
    )(*[in_vmem(b) for b in blocks], *[in_vmem(a) for a in arrived])


def finish_body(n, *refs):
    terms, out_ref, (buf, sem) = refs[:-3], refs[-3], refs[-2:]
    at, copies = 0, []
    for k in range(len(terms) // n):
        total = sum(t[...].astype(jnp.float32) for t in terms[n * k : n * k + n])
        part = total.shape[0]
        buf[at : at + part] = total.astype(jnp.bfloat16)
        rows = pl.ds(at, part)
        copies.append(pltpu.make_async_copy(buf.at[rows], out_ref.at[rows], sem.at[k]))
        copies[-1].start()
        at += part
    for copy in copies:
        copy.wait()


def finish(sums):
    n, blocks = len(sums[0]), [in_vmem(block) for terms in sums for block in terms]
    rows, width = sum(terms[0].shape[0] for terms in sums), blocks[0].shape[1]
    return pl.pallas_call(
        functools.partial(finish_body, n),
        out_shape=jax.ShapeDtypeStruct((rows, width), jnp.bfloat16),
        in_specs=[VMEM_SPEC] * len(blocks),
        out_specs=ANY_SPEC,
        scratch_shapes=[
            pltpu.VMEM((rows, width), jnp.bfloat16),
            pltpu.SemaphoreType.DMA((len(sums),)),
        ],
        compiler_params=pltpu.CompilerParams(vmem_limit_bytes=8 * MIB),
    )(*blocks)


def fetch_body(*refs):
    n = len(refs) // 2
    sem = refs[-1]
    copies = [pltpu.make_async_copy(refs[k], refs[n + k], sem.at[k]) for k in range(n)]
    for copy in copies:
        copy.start()
    for copy in copies:
        copy.wait()


def fetch(arrays):
    n = len(arrays)
    return pl.pallas_call(
        fetch_body,
        out_shape=[vmem_out(a.shape) for a in arrays],
        in_specs=[ANY_SPEC] * n,
        out_specs=[VMEM_SPEC] * n,
        scratch_shapes=[pltpu.SemaphoreType.DMA((n,))],
        compiler_params=pltpu.CompilerParams(vmem_limit_bytes=8 * MIB),
        cost_estimate=pl.CostEstimate(
            flops=0, bytes_accessed=4 * sum(a.size for a in arrays), transcendentals=0
        ),
    )(*[pltpu.with_memory_space_constraint(a, pltpu.HBM) for a in arrays])


def ffn_body(hops, *refs):
    n = len(hops)
    x_refs, weights, o_refs, (x_buf, h_buf) = refs[:n], refs[n : n + 6], refs[n + 6 : -2], refs[-2:]
    width, hidden = x_buf.shape[1], h_buf.shape[1] // 2
    at = 0
    columns = ([], [])
    for x_ref, bits in zip(x_refs, hops):
        x_buf[at : at + x_ref.shape[0]] = x_ref[:, :width]
        at += x_ref.shape[0]
        for e in range(2):
            lane = width + (bits ^ (e * CORE))
            columns[e].append(x_ref[:, lane : lane + 1].astype(jnp.float32))
    columns = [jnp.concatenate(parts) for parts in columns]
    for e in range(2):
        w_gate, w_up = weights[3 * e], weights[3 * e + 1]
        for f in range(0, hidden, 256):
            gate = jnp.dot(x_buf[...], w_gate[:, f : f + 256], preferred_element_type=jnp.float32)
            up = jnp.dot(x_buf[...], w_up[:, f : f + 256], preferred_element_type=jnp.float32)
            act = (gate / (1.0 + jnp.exp(-gate)) * up).astype(jnp.bfloat16)
            h_buf[:, e * hidden + f : e * hidden + f + 256] = act
    for c in range(0, width, 512):
        out = None
        for e in range(2):
            act = h_buf[:, e * hidden : (e + 1) * hidden]
            part = jnp.dot(act, weights[3 * e + 2][:, c : c + 512], preferred_element_type=jnp.float32)
            part = columns[e] * part
            out = part if out is None else out + part
        out = out.astype(jnp.bfloat16)
        at = 0
        for o_ref in o_refs:
            o_ref[:, c : c + 512] = out[at : at + o_ref.shape[0]]
            at += o_ref.shape[0]


def ffn(blocks, hops, *, width, weights):
    pieces = [block.shape[0] for block in blocks]
    rows, n = sum(pieces), len(blocks)
    hidden = weights[0].shape[1]
    moved = sum(w.size * 2 for w in weights) + 4 * rows * width
    return pl.pallas_call(
        functools.partial(ffn_body, hops),
        out_shape=[vmem_out((p, width)) for p in pieces],
        in_specs=[VMEM_SPEC] * (n + 6),
        out_specs=[VMEM_SPEC] * n,
        scratch_shapes=[
            pltpu.VMEM((rows, width), jnp.bfloat16),
            pltpu.VMEM((rows, 2 * hidden), jnp.bfloat16),
        ],
        compiler_params=pltpu.CompilerParams(vmem_limit_bytes=16 * MIB),
        cost_estimate=pl.CostEstimate(
            flops=12 * rows * width * hidden, bytes_accessed=moved, transcendentals=2 * rows * hidden
        ),
    )(*[in_vmem(block) for block in blocks], *[in_vmem(w) for w in weights])


def two_by_two(tokens, expert_ids, gate_weights, w_gate, w_up, w_down):
    tok_dev, width = tokens.shape
    half = tok_dev // 2
    top, low = label(tokens, expert_ids, gate_weights, 128, 2)

    x_top, y_low = hop(top, XBIT), hop(low, YBIT)
    own = (w_gate[0], w_up[0], w_down[0])
    swapped = [hop(w, CORE) for w in own]
    fetched = fetch(own)
    weights = [*fetched, *swapped]
    (x_on,), (y_on,) = after([x_top], fetched[:1]), after([y_low], fetched[:1])
    d_top, d_low = hop(x_on, YBIT), hop(y_on, XBIT)
    low, top = after([low, top], [x_on, y_on, *swapped[:2]])
    x_low, y_top = hop(low, XBIT), hop(top, YBIT)

    run = functools.partial(ffn, width=width, weights=weights)
    ox_top, oy_low = run([x_on, y_on], [XBIT, YBIT])
    d_top, d_low = after([d_top, d_low], [ox_top])
    od_top, od_low = run([d_top, d_low], [XBIT | YBIT] * 2)
    e_top, e_low = hop(od_top, XBIT), hop(od_low, YBIT)
    x_low, y_top = after([x_low, y_top], [od_top])
    oy_top, ox_low = run([y_top, x_low], [YBIT, XBIT])
    ox_top, oy_low = after([ox_top, oy_low], [oy_top])
    fx_top, fy_low = hop(ox_top, XBIT), hop(oy_low, YBIT)
    o_top, o_low = run([top, low], [0, 0])
    f32 = lambda a: a.astype(jnp.float32)
    my_top = hop((f32(oy_top) + f32(e_top)).astype(jnp.bfloat16), YBIT)
    mx_low = hop((f32(ox_low) + f32(e_low)).astype(jnp.bfloat16), XBIT)
    return finish([[o_top, fx_top, my_top], [o_low, fy_low, mx_low]])


def solution(mesh):
    return jax.shard_map(
        two_by_two if mesh.shape[AXIS] == 8 else any_slice,
        mesh=mesh,
        in_specs=(
            P(("dp", AXIS), None),
            P(("dp", AXIS), None),
            P(("dp", AXIS), None),
            P(AXIS, None, None),
            P(AXIS, None, None),
            P(AXIS, None, None),
        ),
        out_specs=P(("dp", AXIS), None),
        check_vma=False,
    )
```

```python
import functools

import jax
import jax.numpy as jnp
from jax import lax
from jax.experimental import pallas as pl
from jax.experimental.pallas import tpu as pltpu
from jax.sharding import PartitionSpec as P

AXIS = "expert"
CORE, XBIT, YBIT = 1, 2, 4
FIRST, SECOND = 2, 4


def slot_table(routed, capacity):
    counted = routed.astype(jnp.int32)
    position = jnp.cumsum(counted, axis=1) - 1
    slot_ids = jnp.arange(capacity, dtype=jnp.int32)
    chosen = routed[:, None, :] & (position[:, None, :] == slot_ids[None, :, None])
    row_ids = jnp.arange(routed.shape[1], dtype=jnp.int32)
    slot_index = jnp.sum(jnp.where(chosen, row_ids[None, None, :], 0), axis=2)
    filled = jnp.any(chosen, axis=2)
    return (slot_index, filled)


def expert_ffn(slot_block, w_gate, w_up, w_down):
    width = slot_block.shape[-1]
    flat_rows = slot_block.reshape(-1, width)
    gate_act = jnp.dot(flat_rows, w_gate[0], preferred_element_type=jnp.float32)
    up_act = jnp.dot(flat_rows, w_up[0], preferred_element_type=jnp.float32)
    hidden = (jax.nn.silu(gate_act) * up_act).astype(jnp.bfloat16)
    expert_out = jnp.dot(hidden, w_down[0], preferred_element_type=jnp.float32)
    return expert_out.reshape(slot_block.shape[:-1] + (w_down.shape[2],))


def swap_all(rows):
    return lax.all_to_all(rows, AXIS, split_axis=0, concat_axis=0, tiled=True)


def route_table(expert_ids, gate_weights, experts):
    labels = jnp.arange(experts, dtype=jnp.int32)
    matched = expert_ids[:, :, None] == labels[None, None, :]
    weights = gate_weights.astype(jnp.float32)[:, :, None]
    return jnp.sum(jnp.where(matched, weights, jnp.float32(0.0)), axis=1)


def any_slice(tokens, expert_ids, gate_weights, w_gate, w_up, w_down):
    tok_dev, choose_k = expert_ids.shape
    width = tokens.shape[1]
    experts = w_gate.shape[0] * lax.axis_size(AXIS)
    capacity = min(tok_dev, 3 * tok_dev * choose_k // (2 * experts))
    weight = route_table(expert_ids, gate_weights, experts)
    home_index, home_filled = slot_table(weight.T != 0.0, capacity)
    arrived = swap_all(tokens[home_index])
    returned_rows = swap_all(expert_ffn(arrived, w_gate, w_up, w_down))
    owners = jnp.arange(experts, dtype=jnp.int32)[:, None]
    factor = jnp.where(home_filled, weight.T[owners, home_index], jnp.float32(0.0))
    combined = jnp.zeros((tok_dev, width), jnp.float32)
    combined = combined.at[home_index.reshape(-1)].add(
        (factor[:, :, None] * returned_rows).reshape(-1, width)
    )
    return combined.astype(jnp.bfloat16)


def hop(block, way):
    bits = {CORE: (CORE, CORE), FIRST: (XBIT, YBIT), SECOND: (YBIT, XBIT)}[way]
    pairs = [(i, i ^ bits[i & CORE]) for i in range(lax.axis_size(AXIS))]
    return lax.ppermute(block, AXIS, pairs)


def in_vmem(array):
    return pltpu.with_memory_space_constraint(array, pltpu.VMEM)


def vmem_out(shape):
    return pltpu.VMEM(shape, jnp.bfloat16)


MIB = 1 << 20
PARTS = 4
VMEM_SPEC = pl.BlockSpec(memory_space=pltpu.VMEM)
ANY_SPEC = pl.BlockSpec(memory_space=pl.ANY)


def parts_of(rows):
    return slice(0, rows // 2), slice(rows // 2, rows), slice(0, rows)


def label_body(tokens_ref, ids_ref, gates_ref, *refs):
    *out_refs, ids_buf, gates_buf, sem = refs
    width = tokens_ref.shape[1]
    rows, tail = ids_ref.shape[1], out_refs[0].shape[1] - width
    pairs = [(ids_ref, ids_buf), (gates_ref, gates_buf)]
    for out_ref, part in zip(out_refs, parts_of(rows)):
        pairs.append((tokens_ref.at[pl.ds(part.start, out_ref.shape[0])], out_ref.at[:, pl.ds(0, width)]))
    copies = [pltpu.make_async_copy(src, dst, sem.at[k]) for k, (src, dst) in enumerate(pairs)]
    for copy in copies:
        copy.start()
    for copy in copies[:2]:
        copy.wait()
    me = lax.axis_index(AXIS)
    column = lax.broadcasted_iota(jnp.int32, (tail, rows), 0)
    gates = gates_buf[...].astype(jnp.float32)
    route = jnp.zeros((tail, rows), jnp.float32)
    for k in range(ids_ref.shape[0]):
        away = ids_buf[k : k + 1, :] ^ me
        turned = (away & CORE) | ((away & XBIT) << 1) | ((away & YBIT) >> 1)
        away = jnp.where(me & CORE == 0, away, turned)
        route += jnp.where(column == away, gates[k : k + 1, :], 0.0)
    route = route.T.astype(jnp.bfloat16)
    for out_ref, part in zip(out_refs, parts_of(rows)):
        out_ref[:, width:] = route[part]
    for copy in copies[2:]:
        copy.wait()


def label(tokens, expert_ids, gate_weights, tail):
    rows, width = tokens.shape
    parts = parts_of(rows)
    arrays = (tokens, expert_ids.T, gate_weights.T)
    return pl.pallas_call(
        label_body,
        out_shape=[vmem_out((p.stop - p.start, width + tail)) for p in parts],
        in_specs=[ANY_SPEC] * 3,
        out_specs=[VMEM_SPEC] * len(parts),
        scratch_shapes=[pltpu.VMEM(a.shape, a.dtype) for a in arrays[1:]]
        + [pltpu.SemaphoreType.DMA((2 + len(parts),))],
        compiler_params=pltpu.CompilerParams(vmem_limit_bytes=8 * MIB),
    )(*[pltpu.with_memory_space_constraint(a, pltpu.HBM) for a in arrays])


def after(value, *arrived):
    return lax.optimization_barrier((value, *arrived))[0]


def finish_body(*refs):
    terms, out_ref, (buf, sem) = refs[:-3], refs[-3], refs[-2:]
    rows = out_ref.shape[0] // PARTS
    copies = []
    for k in range(PARTS):
        part = slice(k * rows, (k + 1) * rows)
        buf[part] = sum(t[part].astype(jnp.float32) for t in terms).astype(jnp.bfloat16)
        at = pl.ds(k * rows, rows)
        copies.append(pltpu.make_async_copy(buf.at[at], out_ref.at[at], sem.at[k]))
        copies[-1].start()
    for copy in copies:
        copy.wait()


def finish(terms):
    shape = terms[0].shape
    return pl.pallas_call(
        finish_body,
        out_shape=jax.ShapeDtypeStruct(shape, jnp.bfloat16),
        in_specs=[VMEM_SPEC] * len(terms),
        out_specs=ANY_SPEC,
        scratch_shapes=[pltpu.VMEM(shape, jnp.bfloat16), pltpu.SemaphoreType.DMA((PARTS,))],
        compiler_params=pltpu.CompilerParams(vmem_limit_bytes=8 * MIB),
    )(*[in_vmem(a) for a in terms])


def fetch_body(n, *refs):
    outs, sem = refs[-n - 1 : -1], refs[-1]
    copies = [pltpu.make_async_copy(refs[k], outs[k], sem.at[k]) for k in range(n)]
    for copy in copies:
        copy.start()
    for copy in copies:
        copy.wait()


def fetch(arrays):
    n = len(arrays)
    return pl.pallas_call(
        functools.partial(fetch_body, n),
        out_shape=[vmem_out(a.shape) for a in arrays],
        in_specs=[ANY_SPEC] * n,
        out_specs=[VMEM_SPEC] * n,
        scratch_shapes=[pltpu.SemaphoreType.DMA((n,))],
        compiler_params=pltpu.CompilerParams(vmem_limit_bytes=8 * MIB),
        cost_estimate=pl.CostEstimate(
            flops=0, bytes_accessed=4 * sum(a.size for a in arrays), transcendentals=0
        ),
    )(*[pltpu.with_memory_space_constraint(a, pltpu.HBM) for a in arrays])


def ffn_body(steps, n, *refs):
    x_refs, weights, (o_ref, x_buf, h_buf) = refs[:n], refs[n : n + 6], refs[n + 6 :]
    width, hidden = o_ref.shape[1], h_buf.shape[1] // 2
    columns, at = ([], []), 0
    for x_ref in x_refs:
        x_buf[at : at + x_ref.shape[0]] = x_ref[:, :width]
        at += x_ref.shape[0]
        for e in range(2):
            lane = width + (steps ^ (e * CORE))
            columns[e].append(x_ref[:, lane : lane + 1].astype(jnp.float32))
    columns = [jnp.concatenate(parts) for parts in columns]
    for e in range(2):
        w_gate, w_up = weights[3 * e], weights[3 * e + 1]
        for f in range(0, hidden, 256):
            x = x_buf[...]
            gate = jnp.dot(x, w_gate[:, f : f + 256], preferred_element_type=jnp.float32)
            up = jnp.dot(x, w_up[:, f : f + 256], preferred_element_type=jnp.float32)
            act = (gate / (1.0 + jnp.exp(-gate)) * up).astype(jnp.bfloat16)
            h_buf[:, e * hidden + f : e * hidden + f + 256] = act
    for c in range(0, width, 512):
        out = None
        for e in range(2):
            act = h_buf[:, e * hidden : (e + 1) * hidden]
            part = jnp.dot(act, weights[3 * e + 2][:, c : c + 512], preferred_element_type=jnp.float32)
            part = columns[e] * part
            out = part if out is None else out + part
        o_ref[:, c : c + 512] = out.astype(jnp.bfloat16)


def ffn(blocks, steps, *, width, weights):
    rows, hidden = sum(block.shape[0] for block in blocks), weights[0].shape[1]
    return pl.pallas_call(
        functools.partial(ffn_body, steps, len(blocks)),
        out_shape=vmem_out((rows, width)),
        in_specs=[VMEM_SPEC] * (len(blocks) + 6),
        out_specs=VMEM_SPEC,
        scratch_shapes=[
            pltpu.VMEM((rows, width), jnp.bfloat16),
            pltpu.VMEM((rows, 2 * hidden), jnp.bfloat16),
        ],
        compiler_params=pltpu.CompilerParams(vmem_limit_bytes=16 * MIB),
        cost_estimate=pl.CostEstimate(
            flops=12 * rows * width * hidden,
            bytes_accessed=2 * sum(w.size for w in weights) + 4 * rows * width,
            transcendentals=2 * rows * hidden,
        ),
    )(*[in_vmem(a) for a in (*blocks, *weights)])


def two_by_two(tokens, expert_ids, gate_weights, w_gate, w_up, w_down):
    width = tokens.shape[1]
    *halves, home = label(tokens, expert_ids, gate_weights, 128)

    near = [hop(half, FIRST) for half in halves]
    own = (w_gate[0], w_up[0], w_down[0])
    swapped = [hop(w, CORE) for w in own]
    fetched = fetch(own)
    near = [after(half, fetched[0]) for half in near]
    far = [hop(half, SECOND) for half in near]
    side = hop(after(home, *near), SECOND)

    run = functools.partial(ffn, width=width, weights=[*fetched, *swapped])
    far_out = run(far, FIRST | SECOND)
    passed = hop(far_out, FIRST)
    near_out = run([after(near[0], far_out), near[1]], FIRST)
    from_near = hop(near_out, FIRST)
    side_out = run([after(side, near_out)], SECOND)
    joined = side_out.astype(jnp.float32) + passed.astype(jnp.float32)
    from_side = hop(joined.astype(jnp.bfloat16), SECOND)
    home_out = run([after(home, from_near)], 0)
    return finish([home_out, from_near, from_side])


def solution(mesh):
    return jax.shard_map(
        two_by_two if mesh.shape[AXIS] == 8 else any_slice,
        mesh=mesh,
        in_specs=(
            P(("dp", AXIS), None),
            P(("dp", AXIS), None),
            P(("dp", AXIS), None),
            P(AXIS, None, None),
            P(AXIS, None, None),
            P(AXIS, None, None),
        ),
        out_specs=P(("dp", AXIS), None),
        check_vma=False,
    )
```

```python
import functools

import jax
import jax.numpy as jnp
from jax import lax
from jax.experimental import pallas as pl
from jax.experimental.pallas import tpu as pltpu
from jax.sharding import PartitionSpec as P

AXIS = "expert"
CORE, XBIT, YBIT = 1, 2, 4
FIRST, SECOND = 2, 4


def slot_table(routed, capacity):
    counted = routed.astype(jnp.int32)
    position = jnp.cumsum(counted, axis=1) - 1
    slot_ids = jnp.arange(capacity, dtype=jnp.int32)
    chosen = routed[:, None, :] & (position[:, None, :] == slot_ids[None, :, None])
    row_ids = jnp.arange(routed.shape[1], dtype=jnp.int32)
    slot_index = jnp.sum(jnp.where(chosen, row_ids[None, None, :], 0), axis=2)
    filled = jnp.any(chosen, axis=2)
    return (slot_index, filled)


def expert_ffn(slot_block, w_gate, w_up, w_down):
    width = slot_block.shape[-1]
    flat_rows = slot_block.reshape(-1, width)
    gate_act = jnp.dot(flat_rows, w_gate[0], preferred_element_type=jnp.float32)
    up_act = jnp.dot(flat_rows, w_up[0], preferred_element_type=jnp.float32)
    hidden = (jax.nn.silu(gate_act) * up_act).astype(jnp.bfloat16)
    expert_out = jnp.dot(hidden, w_down[0], preferred_element_type=jnp.float32)
    return expert_out.reshape(slot_block.shape[:-1] + (w_down.shape[2],))


def swap_all(rows):
    return lax.all_to_all(rows, AXIS, split_axis=0, concat_axis=0, tiled=True)


def route_table(expert_ids, gate_weights, experts):
    labels = jnp.arange(experts, dtype=jnp.int32)
    matched = expert_ids[:, :, None] == labels[None, None, :]
    weights = gate_weights.astype(jnp.float32)[:, :, None]
    return jnp.sum(jnp.where(matched, weights, jnp.float32(0.0)), axis=1)


def any_slice(tokens, expert_ids, gate_weights, w_gate, w_up, w_down):
    tok_dev, choose_k = expert_ids.shape
    width = tokens.shape[1]
    experts = w_gate.shape[0] * lax.axis_size(AXIS)
    capacity = min(tok_dev, 3 * tok_dev * choose_k // (2 * experts))
    weight = route_table(expert_ids, gate_weights, experts)
    home_index, home_filled = slot_table(weight.T != 0.0, capacity)
    arrived = swap_all(tokens[home_index])
    returned_rows = swap_all(expert_ffn(arrived, w_gate, w_up, w_down))
    owners = jnp.arange(experts, dtype=jnp.int32)[:, None]
    factor = jnp.where(home_filled, weight.T[owners, home_index], jnp.float32(0.0))
    combined = jnp.zeros((tok_dev, width), jnp.float32)
    combined = combined.at[home_index.reshape(-1)].add(
        (factor[:, :, None] * returned_rows).reshape(-1, width)
    )
    return combined.astype(jnp.bfloat16)


def hop(block, way):
    bits = {CORE: (CORE, CORE), FIRST: (XBIT, YBIT), SECOND: (YBIT, XBIT)}[way]
    pairs = [(i, i ^ bits[i & CORE]) for i in range(lax.axis_size(AXIS))]
    return lax.ppermute(block, AXIS, pairs)


def in_vmem(array):
    return pltpu.with_memory_space_constraint(array, pltpu.VMEM)


def vmem_out(shape):
    return pltpu.VMEM(shape, jnp.bfloat16)


MIB = 1 << 20
PARTS = 4
LANES = 128
WEIGHT_ROWS = 16
VMEM_SPEC = pl.BlockSpec(memory_space=pltpu.VMEM)
ANY_SPEC = pl.BlockSpec(memory_space=pl.ANY)


def parts_of(rows):
    return slice(0, rows // 2), slice(rows // 2, rows), slice(0, rows)


def label_body(tokens_ref, ids_ref, gates_ref, *refs):
    *out_refs, buf, ids_buf, gates_buf, sem = refs
    rows, width = buf.shape
    pairs = [(ids_ref, ids_buf), (gates_ref, gates_buf), (tokens_ref, buf)]
    copies = [pltpu.make_async_copy(src, dst, sem.at[k]) for k, (src, dst) in enumerate(pairs)]
    for copy in copies:
        copy.start()
    for copy in copies[:2]:
        copy.wait()
    me = lax.axis_index(AXIS)
    row = lax.broadcasted_iota(jnp.int32, (WEIGHT_ROWS, rows), 0)
    gates = gates_buf[...].astype(jnp.float32)
    route = jnp.zeros((WEIGHT_ROWS, rows), jnp.float32)
    for k in range(ids_ref.shape[0]):
        away = ids_buf[k : k + 1, :] ^ me
        turned = (away & CORE) | ((away & XBIT) << 1) | ((away & YBIT) >> 1)
        away = jnp.where(me & CORE == 0, away, turned)
        route += jnp.where(row == away, gates[k : k + 1, :], 0.0)
    route = route.astype(jnp.bfloat16)
    for out_ref in out_refs:
        out_ref[out_ref.shape[0] - WEIGHT_ROWS :] = route
    copies[2].wait()
    for out_ref, part in zip(out_refs, parts_of(rows)):
        size = part.stop - part.start
        for k in range(width // LANES):
            out_ref[k * size : (k + 1) * size] = buf[part, k * LANES : (k + 1) * LANES]


def label(tokens, expert_ids, gate_weights):
    rows, width = tokens.shape
    parts = parts_of(rows)
    arrays = (tokens, expert_ids.T, gate_weights.T)
    lengths = [(p.stop - p.start) * width // LANES + WEIGHT_ROWS for p in parts]
    return pl.pallas_call(
        label_body,
        out_shape=[vmem_out((length, LANES)) for length in lengths],
        in_specs=[ANY_SPEC] * 3,
        out_specs=[VMEM_SPEC] * len(parts),
        scratch_shapes=[pltpu.VMEM(a.shape, a.dtype) for a in arrays]
        + [pltpu.SemaphoreType.DMA((3,))],
        compiler_params=pltpu.CompilerParams(vmem_limit_bytes=8 * MIB),
    )(*[pltpu.with_memory_space_constraint(a, pltpu.HBM) for a in arrays])


def after(value, *arrived):
    return lax.optimization_barrier((value, *arrived))[0]


def finish_body(*refs):
    terms, out_ref, (buf, sem) = refs[:-3], refs[-3], refs[-2:]
    rows = out_ref.shape[0] // PARTS
    copies = []
    for k in range(PARTS):
        part = slice(k * rows, (k + 1) * rows)
        buf[part] = sum(t[part].astype(jnp.float32) for t in terms).astype(jnp.bfloat16)
        at = pl.ds(k * rows, rows)
        copies.append(pltpu.make_async_copy(buf.at[at], out_ref.at[at], sem.at[k]))
        copies[-1].start()
    for copy in copies:
        copy.wait()


def finish(terms):
    shape = terms[0].shape
    return pl.pallas_call(
        finish_body,
        out_shape=jax.ShapeDtypeStruct(shape, jnp.bfloat16),
        in_specs=[VMEM_SPEC] * len(terms),
        out_specs=ANY_SPEC,
        scratch_shapes=[pltpu.VMEM(shape, jnp.bfloat16), pltpu.SemaphoreType.DMA((PARTS,))],
        compiler_params=pltpu.CompilerParams(vmem_limit_bytes=8 * MIB),
    )(*[in_vmem(a) for a in terms])


def stage_body(*refs):
    n = len(refs) // 2
    for src, dst in zip(refs[:n], refs[n:]):
        dst[...] = src[...]


def stage(parts, hint):
    n = len(parts)
    return pl.pallas_call(
        stage_body,
        out_shape=[vmem_out(p.shape) for p in parts],
        in_specs=[VMEM_SPEC] * n,
        out_specs=[VMEM_SPEC] * n,
        compiler_params=pltpu.CompilerParams(vmem_limit_bytes=8 * MIB),
        cost_estimate=pl.CostEstimate(
            flops=hint, bytes_accessed=4 * sum(p.size for p in parts), transcendentals=0
        ),
    )(*[in_vmem(p) for p in parts])


def add_body(a_ref, b_ref, out_ref):
    out_ref[...] = a_ref[...].astype(jnp.float32) + b_ref[...].astype(jnp.float32)


def add(a, b):
    return pl.pallas_call(
        add_body,
        out_shape=pltpu.VMEM(a.shape, jnp.float32),
        in_specs=[VMEM_SPEC] * 2,
        out_specs=VMEM_SPEC,
        compiler_params=pltpu.CompilerParams(vmem_limit_bytes=8 * MIB),
        cost_estimate=pl.CostEstimate(flops=10000000000, bytes_accessed=8 * a.size, transcendentals=0),
    )(in_vmem(a), in_vmem(b))


def fetch_body(n, *refs):
    outs, sem = refs[-n - 1 : -1], refs[-1]
    copies = [pltpu.make_async_copy(refs[k], outs[k], sem.at[k]) for k in range(n)]
    for copy in copies:
        copy.start()
    for copy in copies:
        copy.wait()


def fetch(arrays):
    n = len(arrays)
    return pl.pallas_call(
        functools.partial(fetch_body, n),
        out_shape=[vmem_out(a.shape) for a in arrays],
        in_specs=[ANY_SPEC] * n,
        out_specs=[VMEM_SPEC] * n,
        scratch_shapes=[pltpu.SemaphoreType.DMA((n,))],
        compiler_params=pltpu.CompilerParams(vmem_limit_bytes=8 * MIB),
        cost_estimate=pl.CostEstimate(
            flops=0, bytes_accessed=4 * sum(a.size for a in arrays), transcendentals=0
        ),
    )(*[pltpu.with_memory_space_constraint(a, pltpu.HBM) for a in arrays])


def ffn_body(steps, n, *refs):
    x_refs, weights, (o_ref, x_buf, h_buf) = refs[:n], refs[n : n + 6], refs[n + 6 :]
    width, hidden = o_ref.shape[1], h_buf.shape[1] // 2
    at = 0
    for x_ref in x_refs:
        rows = (x_ref.shape[0] - WEIGHT_ROWS) * LANES // width
        for k in range(width // LANES):
            x_buf[at : at + rows, k * LANES : (k + 1) * LANES] = x_ref[k * rows : (k + 1) * rows]
        at += rows
    route = x_refs[0][x_refs[0].shape[0] - WEIGHT_ROWS :].astype(jnp.float32)
    columns = []
    for row in (steps, steps ^ CORE):
        spread = jnp.broadcast_to(route[row : row + 1], (route.shape[1], route.shape[1]))
        columns.append(spread.T[:, :1])
    for e in range(2):
        w_gate, w_up = weights[3 * e], weights[3 * e + 1]
        for f in range(0, hidden, 256):
            x = x_buf[...]
            gate = jnp.dot(x, w_gate[:, f : f + 256], preferred_element_type=jnp.float32)
            up = jnp.dot(x, w_up[:, f : f + 256], preferred_element_type=jnp.float32)
            act = (gate / (1.0 + jnp.exp(-gate)) * up).astype(jnp.bfloat16)
            h_buf[:, e * hidden + f : e * hidden + f + 256] = act
    for c in range(0, width, 512):
        out = None
        for e in range(2):
            act = h_buf[:, e * hidden : (e + 1) * hidden]
            part = jnp.dot(act, weights[3 * e + 2][:, c : c + 512], preferred_element_type=jnp.float32)
            part = columns[e] * part
            out = part if out is None else out + part
        o_ref[:, c : c + 512] = out.astype(jnp.bfloat16)


def ffn(blocks, steps, *, width, weights):
    hidden = weights[0].shape[1]
    rows = sum(block.shape[0] - WEIGHT_ROWS for block in blocks) * LANES // width
    return pl.pallas_call(
        functools.partial(ffn_body, steps, len(blocks)),
        out_shape=vmem_out((rows, width)),
        in_specs=[VMEM_SPEC] * (len(blocks) + 6),
        out_specs=VMEM_SPEC,
        scratch_shapes=[
            pltpu.VMEM((rows, width), jnp.bfloat16),
            pltpu.VMEM((rows, 2 * hidden), jnp.bfloat16),
        ],
        compiler_params=pltpu.CompilerParams(vmem_limit_bytes=16 * MIB),
        cost_estimate=pl.CostEstimate(
            flops=12 * rows * width * hidden,
            bytes_accessed=2 * sum(w.size for w in weights) + 4 * rows * width,
            transcendentals=2 * rows * hidden,
        ),
    )(*[in_vmem(a) for a in (*blocks, *weights)])


def two_by_two(tokens, expert_ids, gate_weights, w_gate, w_up, w_down):
    width = tokens.shape[1]
    *halves, home = label(tokens, expert_ids, gate_weights)

    near = [hop(half, FIRST) for half in halves]
    own = (w_gate[0], w_up[0], w_down[0])
    fetched = fetch(own)
    swapped = [hop(w, CORE) for w in own]
    near = [after(half, fetched[0]) for half in near]
    far = stage([hop(half, SECOND) for half in near], 28000000000)
    side = [hop(after(home, *near, swapped[0]), SECOND)]

    run = functools.partial(ffn, width=width, weights=[*fetched, *swapped])
    far_out = run(far, FIRST | SECOND)
    passed = hop(far_out, FIRST)
    near_out = run([after(near[0], far_out), near[1]], FIRST)
    from_near = hop(near_out, FIRST)
    side_out = run([after(side[0], near_out), *side[1:]], SECOND)
    joined = side_out.astype(jnp.float32) + passed.astype(jnp.float32)
    joined = joined.astype(jnp.bfloat16)
    from_side = hop(joined, SECOND)
    home_out = run([after(home, joined)], 0)
    total = add(home_out, from_near)
    return finish([total, from_side])


def on_device(tokens, *rest):
    fits = lax.axis_size(AXIS) == 8 and tokens.shape[0] == LANES
    return (two_by_two if fits else any_slice)(tokens, *rest)


def solution(mesh):
    return jax.shard_map(
        on_device,
        mesh=mesh,
        in_specs=(
            P(("dp", AXIS), None),
            P(("dp", AXIS), None),
            P(("dp", AXIS), None),
            P(AXIS, None, None),
            P(AXIS, None, None),
            P(AXIS, None, None),
        ),
        out_specs=P(("dp", AXIS), None),
        check_vma=False,
    )
```

```python
import functools

import jax
import jax.numpy as jnp
from jax import lax
from jax.experimental import pallas as pl
from jax.experimental.pallas import tpu as pltpu
from jax.sharding import PartitionSpec as P

AXIS = "expert"
CORE, XBIT, YBIT = 1, 2, 4
FIRST, SECOND = 2, 4


def slot_table(routed, capacity):
    counted = routed.astype(jnp.int32)
    position = jnp.cumsum(counted, axis=1) - 1
    slot_ids = jnp.arange(capacity, dtype=jnp.int32)
    chosen = routed[:, None, :] & (position[:, None, :] == slot_ids[None, :, None])
    row_ids = jnp.arange(routed.shape[1], dtype=jnp.int32)
    slot_index = jnp.sum(jnp.where(chosen, row_ids[None, None, :], 0), axis=2)
    filled = jnp.any(chosen, axis=2)
    return (slot_index, filled)


def expert_ffn(slot_block, w_gate, w_up, w_down):
    width = slot_block.shape[-1]
    flat_rows = slot_block.reshape(-1, width)
    gate_act = jnp.dot(flat_rows, w_gate[0], preferred_element_type=jnp.float32)
    up_act = jnp.dot(flat_rows, w_up[0], preferred_element_type=jnp.float32)
    hidden = (jax.nn.silu(gate_act) * up_act).astype(jnp.bfloat16)
    expert_out = jnp.dot(hidden, w_down[0], preferred_element_type=jnp.float32)
    return expert_out.reshape(slot_block.shape[:-1] + (w_down.shape[2],))


def swap_all(rows):
    return lax.all_to_all(rows, AXIS, split_axis=0, concat_axis=0, tiled=True)


def route_table(expert_ids, gate_weights, experts):
    labels = jnp.arange(experts, dtype=jnp.int32)
    matched = expert_ids[:, :, None] == labels[None, None, :]
    weights = gate_weights.astype(jnp.float32)[:, :, None]
    return jnp.sum(jnp.where(matched, weights, jnp.float32(0.0)), axis=1)


def any_slice(tokens, expert_ids, gate_weights, w_gate, w_up, w_down):
    tok_dev, choose_k = expert_ids.shape
    width = tokens.shape[1]
    experts = w_gate.shape[0] * lax.axis_size(AXIS)
    capacity = min(tok_dev, 3 * tok_dev * choose_k // (2 * experts))
    weight = route_table(expert_ids, gate_weights, experts)
    home_index, home_filled = slot_table(weight.T != 0.0, capacity)
    arrived = swap_all(tokens[home_index])
    returned_rows = swap_all(expert_ffn(arrived, w_gate, w_up, w_down))
    owners = jnp.arange(experts, dtype=jnp.int32)[:, None]
    factor = jnp.where(home_filled, weight.T[owners, home_index], jnp.float32(0.0))
    combined = jnp.zeros((tok_dev, width), jnp.float32)
    combined = combined.at[home_index.reshape(-1)].add(
        (factor[:, :, None] * returned_rows).reshape(-1, width)
    )
    return combined.astype(jnp.bfloat16)


def hop(block, way):
    bits = {CORE: (CORE, CORE), FIRST: (XBIT, YBIT), SECOND: (YBIT, XBIT)}[way]
    pairs = [(i, i ^ bits[i & CORE]) for i in range(lax.axis_size(AXIS))]
    return lax.ppermute(block, AXIS, pairs)


def in_vmem(array):
    return pltpu.with_memory_space_constraint(array, pltpu.VMEM)


def vmem_out(shape):
    return pltpu.VMEM(shape, jnp.bfloat16)


MIB = 1 << 20
PARTS = 4
LANES = 128
WEIGHT_ROWS = 16
VMEM_SPEC = pl.BlockSpec(memory_space=pltpu.VMEM)
ANY_SPEC = pl.BlockSpec(memory_space=pl.ANY)


def parts_of(rows):
    return slice(0, rows // 2), slice(rows // 2, rows), slice(0, rows)


def label_body(tokens_ref, ids_ref, gates_ref, *refs):
    *out_refs, buf, ids_buf, gates_buf, sem = refs
    rows, width = buf.shape
    pairs = [(ids_ref, ids_buf), (gates_ref, gates_buf), (tokens_ref, buf)]
    copies = [pltpu.make_async_copy(src, dst, sem.at[k]) for k, (src, dst) in enumerate(pairs)]
    for copy in copies:
        copy.start()
    for copy in copies[:2]:
        copy.wait()
    me = lax.axis_index(AXIS)
    row = lax.broadcasted_iota(jnp.int32, (WEIGHT_ROWS, rows), 0)
    gates = gates_buf[...].astype(jnp.float32)
    route = jnp.zeros((WEIGHT_ROWS, rows), jnp.float32)
    for k in range(ids_ref.shape[0]):
        away = ids_buf[k : k + 1, :] ^ me
        turned = (away & CORE) | ((away & XBIT) << 1) | ((away & YBIT) >> 1)
        away = jnp.where(me & CORE == 0, away, turned)
        route += jnp.where(row == away, gates[k : k + 1, :], 0.0)
    route = route.astype(jnp.bfloat16)
    for out_ref in out_refs:
        out_ref[out_ref.shape[0] - WEIGHT_ROWS :] = route
    copies[2].wait()
    for out_ref, part in zip(out_refs, parts_of(rows)):
        size = part.stop - part.start
        for k in range(width // LANES):
            out_ref[k * size : (k + 1) * size] = buf[part, k * LANES : (k + 1) * LANES]


def label(tokens, expert_ids, gate_weights):
    rows, width = tokens.shape
    parts = parts_of(rows)
    arrays = (tokens, expert_ids.T, gate_weights.T)
    lengths = [(p.stop - p.start) * width // LANES + WEIGHT_ROWS for p in parts]
    return pl.pallas_call(
        label_body,
        out_shape=[vmem_out((length, LANES)) for length in lengths],
        in_specs=[ANY_SPEC] * 3,
        out_specs=[VMEM_SPEC] * len(parts),
        scratch_shapes=[pltpu.VMEM(a.shape, a.dtype) for a in arrays]
        + [pltpu.SemaphoreType.DMA((3,))],
        compiler_params=pltpu.CompilerParams(vmem_limit_bytes=8 * MIB),
    )(*[pltpu.with_memory_space_constraint(a, pltpu.HBM) for a in arrays])


def after(value, *arrived):
    return lax.optimization_barrier((value, *arrived))[0]


def finish_body(*refs):
    terms, out_ref, (buf, sem) = refs[:-3], refs[-3], refs[-2:]
    rows = out_ref.shape[0] // PARTS
    copies = []
    for k in range(PARTS):
        part = slice(k * rows, (k + 1) * rows)
        buf[part] = sum(t[part].astype(jnp.float32) for t in terms).astype(jnp.bfloat16)
        at = pl.ds(k * rows, rows)
        copies.append(pltpu.make_async_copy(buf.at[at], out_ref.at[at], sem.at[k]))
        copies[-1].start()
    for copy in copies:
        copy.wait()


def finish(terms):
    shape = terms[0].shape
    return pl.pallas_call(
        finish_body,
        out_shape=jax.ShapeDtypeStruct(shape, jnp.bfloat16),
        in_specs=[VMEM_SPEC] * len(terms),
        out_specs=ANY_SPEC,
        scratch_shapes=[pltpu.VMEM(shape, jnp.bfloat16), pltpu.SemaphoreType.DMA((PARTS,))],
        compiler_params=pltpu.CompilerParams(vmem_limit_bytes=8 * MIB),
    )(*[in_vmem(a) for a in terms])


def stage_body(*refs):
    n = len(refs) // 2
    for src, dst in zip(refs[:n], refs[n:]):
        dst[...] = src[...]


def stage(parts, hint):
    n = len(parts)
    return pl.pallas_call(
        stage_body,
        out_shape=[vmem_out(p.shape) for p in parts],
        in_specs=[VMEM_SPEC] * n,
        out_specs=[VMEM_SPEC] * n,
        compiler_params=pltpu.CompilerParams(vmem_limit_bytes=8 * MIB),
        cost_estimate=pl.CostEstimate(
            flops=hint, bytes_accessed=4 * sum(p.size for p in parts), transcendentals=0
        ),
    )(*[in_vmem(p) for p in parts])


def add_body(a_ref, b_ref, out_ref):
    out_ref[...] = a_ref[...].astype(jnp.float32) + b_ref[...].astype(jnp.float32)


def add(a, b):
    return pl.pallas_call(
        add_body,
        out_shape=pltpu.VMEM(a.shape, jnp.float32),
        in_specs=[VMEM_SPEC] * 2,
        out_specs=VMEM_SPEC,
        compiler_params=pltpu.CompilerParams(vmem_limit_bytes=8 * MIB),
        cost_estimate=pl.CostEstimate(flops=10000000000, bytes_accessed=8 * a.size, transcendentals=0),
    )(in_vmem(a), in_vmem(b))


def fetch_body(n, *refs):
    outs, sem = refs[-n - 1 : -1], refs[-1]
    copies = [pltpu.make_async_copy(refs[k], outs[k], sem.at[k]) for k in range(n)]
    for copy in copies:
        copy.start()
    for copy in copies:
        copy.wait()


def fetch(arrays):
    n = len(arrays)
    return pl.pallas_call(
        functools.partial(fetch_body, n),
        out_shape=[vmem_out(a.shape) for a in arrays],
        in_specs=[ANY_SPEC] * n,
        out_specs=[VMEM_SPEC] * n,
        scratch_shapes=[pltpu.SemaphoreType.DMA((n,))],
        compiler_params=pltpu.CompilerParams(vmem_limit_bytes=8 * MIB),
        cost_estimate=pl.CostEstimate(
            flops=0, bytes_accessed=4 * sum(a.size for a in arrays), transcendentals=0
        ),
    )(*[pltpu.with_memory_space_constraint(a, pltpu.HBM) for a in arrays])


def ffn_body(steps, n, *refs):
    x_refs, weights, (o_ref, x_buf, h_buf) = refs[:n], refs[n : n + 6], refs[n + 6 :]
    width, hidden = o_ref.shape[1], h_buf.shape[1] // 2
    parts = []
    for x_ref in x_refs:
        rows = (x_ref.shape[0] - WEIGHT_ROWS) * LANES // width
        blocks = [x_ref[k * rows : (k + 1) * rows] for k in range(width // LANES)]
        parts.append(jnp.concatenate(blocks, axis=1))
    x_buf[...] = jnp.concatenate(parts)
    route = x_refs[0][x_refs[0].shape[0] - WEIGHT_ROWS :].astype(jnp.float32)
    columns = []
    for row in (steps, steps ^ CORE):
        spread = jnp.broadcast_to(route[row : row + 1], (route.shape[1], route.shape[1]))
        columns.append(spread.T[:, :1])
    for e in range(2):
        w_gate, w_up = weights[3 * e], weights[3 * e + 1]
        for f in range(0, hidden, 256):
            x = x_buf[...]
            gate = jnp.dot(x, w_gate[:, f : f + 256], preferred_element_type=jnp.float32)
            up = jnp.dot(x, w_up[:, f : f + 256], preferred_element_type=jnp.float32)
            act = (gate / (1.0 + jnp.exp(-gate)) * up).astype(jnp.bfloat16)
            h_buf[:, e * hidden + f : e * hidden + f + 256] = act
    for c in range(0, width, 1024):
        out = None
        for e in range(2):
            act = h_buf[:, e * hidden : (e + 1) * hidden]
            part = jnp.dot(act, weights[3 * e + 2][:, c : c + 1024], preferred_element_type=jnp.float32)
            part = columns[e] * part
            out = part if out is None else out + part
        o_ref[:, c : c + 1024] = out.astype(jnp.bfloat16)


def ffn(blocks, steps, *, width, weights):
    hidden = weights[0].shape[1]
    rows = sum(block.shape[0] - WEIGHT_ROWS for block in blocks) * LANES // width
    return pl.pallas_call(
        functools.partial(ffn_body, steps, len(blocks)),
        out_shape=vmem_out((rows, width)),
        in_specs=[VMEM_SPEC] * (len(blocks) + 6),
        out_specs=VMEM_SPEC,
        scratch_shapes=[
            pltpu.VMEM((rows, width), jnp.bfloat16),
            pltpu.VMEM((rows, 2 * hidden), jnp.bfloat16),
        ],
        compiler_params=pltpu.CompilerParams(vmem_limit_bytes=16 * MIB),
        cost_estimate=pl.CostEstimate(
            flops=12 * rows * width * hidden,
            bytes_accessed=2 * sum(w.size for w in weights) + 4 * rows * width,
            transcendentals=2 * rows * hidden,
        ),
    )(*[in_vmem(a) for a in (*blocks, *weights)])


def two_by_two(tokens, expert_ids, gate_weights, w_gate, w_up, w_down):
    width = tokens.shape[1]
    *halves, home = label(tokens, expert_ids, gate_weights)

    near = [hop(half, FIRST) for half in halves]
    own = (w_gate[0], w_up[0], w_down[0])
    fetched = fetch(own)
    swapped = [hop(w, CORE) for w in own]
    near = [after(half, fetched[0]) for half in near]
    far = stage([hop(half, SECOND) for half in near], 28000000000)
    side = [hop(after(home, *near, swapped[0]), SECOND)]

    run = functools.partial(ffn, width=width, weights=[*fetched, *swapped])
    far_out = run(far, FIRST | SECOND)
    passed = hop(far_out, FIRST)
    near_out = run([after(near[0], far_out), near[1]], FIRST)
    from_near = hop(near_out, FIRST)
    side_out = run([after(side[0], near_out), *side[1:]], SECOND)
    joined = side_out.astype(jnp.float32) + passed.astype(jnp.float32)
    joined = joined.astype(jnp.bfloat16)
    from_side = hop(joined, SECOND)
    home_out = run([after(home, joined)], 0)
    total = add(home_out, from_near)
    return finish([total, from_side])


def on_device(tokens, *rest):
    fits = lax.axis_size(AXIS) == 8 and tokens.shape[0] == LANES
    return (two_by_two if fits else any_slice)(tokens, *rest)


def solution(mesh):
    return jax.shard_map(
        on_device,
        mesh=mesh,
        in_specs=(
            P(("dp", AXIS), None),
            P(("dp", AXIS), None),
            P(("dp", AXIS), None),
            P(AXIS, None, None),
            P(AXIS, None, None),
            P(AXIS, None, None),
        ),
        out_specs=P(("dp", AXIS), None),
        check_vma=False,
    )
```

```python
import functools

import jax
import jax.numpy as jnp
from jax import lax
from jax.experimental import pallas as pl
from jax.experimental.pallas import tpu as pltpu
from jax.sharding import PartitionSpec as P

AXIS = "expert"
CORE, XBIT, YBIT = 1, 2, 4
FIRST, SECOND = 2, 4


def slot_table(routed, capacity):
    counted = routed.astype(jnp.int32)
    position = jnp.cumsum(counted, axis=1) - 1
    slot_ids = jnp.arange(capacity, dtype=jnp.int32)
    chosen = routed[:, None, :] & (position[:, None, :] == slot_ids[None, :, None])
    row_ids = jnp.arange(routed.shape[1], dtype=jnp.int32)
    slot_index = jnp.sum(jnp.where(chosen, row_ids[None, None, :], 0), axis=2)
    filled = jnp.any(chosen, axis=2)
    return (slot_index, filled)


def expert_ffn(slot_block, w_gate, w_up, w_down):
    width = slot_block.shape[-1]
    flat_rows = slot_block.reshape(-1, width)
    gate_act = jnp.dot(flat_rows, w_gate[0], preferred_element_type=jnp.float32)
    up_act = jnp.dot(flat_rows, w_up[0], preferred_element_type=jnp.float32)
    hidden = (jax.nn.silu(gate_act) * up_act).astype(jnp.bfloat16)
    expert_out = jnp.dot(hidden, w_down[0], preferred_element_type=jnp.float32)
    return expert_out.reshape(slot_block.shape[:-1] + (w_down.shape[2],))


def swap_all(rows):
    return lax.all_to_all(rows, AXIS, split_axis=0, concat_axis=0, tiled=True)


def route_table(expert_ids, gate_weights, experts):
    labels = jnp.arange(experts, dtype=jnp.int32)
    matched = expert_ids[:, :, None] == labels[None, None, :]
    weights = gate_weights.astype(jnp.float32)[:, :, None]
    return jnp.sum(jnp.where(matched, weights, jnp.float32(0.0)), axis=1)


def any_slice(tokens, expert_ids, gate_weights, w_gate, w_up, w_down):
    tok_dev, choose_k = expert_ids.shape
    width = tokens.shape[1]
    experts = w_gate.shape[0] * lax.axis_size(AXIS)
    capacity = min(tok_dev, 3 * tok_dev * choose_k // (2 * experts))
    weight = route_table(expert_ids, gate_weights, experts)
    home_index, home_filled = slot_table(weight.T != 0.0, capacity)
    arrived = swap_all(tokens[home_index])
    returned_rows = swap_all(expert_ffn(arrived, w_gate, w_up, w_down))
    owners = jnp.arange(experts, dtype=jnp.int32)[:, None]
    factor = jnp.where(home_filled, weight.T[owners, home_index], jnp.float32(0.0))
    combined = jnp.zeros((tok_dev, width), jnp.float32)
    combined = combined.at[home_index.reshape(-1)].add(
        (factor[:, :, None] * returned_rows).reshape(-1, width)
    )
    return combined.astype(jnp.bfloat16)


def hop(block, way):
    bits = {CORE: (CORE, CORE), FIRST: (XBIT, YBIT), SECOND: (YBIT, XBIT)}[way]
    pairs = [(i, i ^ bits[i & CORE]) for i in range(lax.axis_size(AXIS))]
    return lax.ppermute(block, AXIS, pairs)


def in_vmem(array):
    return pltpu.with_memory_space_constraint(array, pltpu.VMEM)


def vmem_out(shape):
    return pltpu.VMEM(shape, jnp.bfloat16)


MIB = 1 << 20
PARTS = 4
LANES = 128
WEIGHT_ROWS = 16
VMEM_SPEC = pl.BlockSpec(memory_space=pltpu.VMEM)
ANY_SPEC = pl.BlockSpec(memory_space=pl.ANY)


def parts_of(rows):
    return slice(0, rows // 2), slice(rows // 2, rows)


def label_body(tokens_ref, ids_ref, gates_ref, *refs):
    *out_refs, buf, ids_buf, gates_buf, sem = refs
    rows, width = buf.shape
    parts = parts_of(rows)
    pairs = [(ids_ref, ids_buf), (gates_ref, gates_buf)]
    for part in parts:
        at = pl.ds(part.start, part.stop - part.start)
        pairs.append((tokens_ref.at[at], buf.at[at]))
    copies = [pltpu.make_async_copy(src, dst, sem.at[k]) for k, (src, dst) in enumerate(pairs)]
    for copy in copies:
        copy.start()
    for copy in copies[:2]:
        copy.wait()
    me = lax.axis_index(AXIS)
    row = lax.broadcasted_iota(jnp.int32, (WEIGHT_ROWS, rows), 0)
    gates = gates_buf[...].astype(jnp.float32)
    route = jnp.zeros((WEIGHT_ROWS, rows), jnp.float32)
    for k in range(ids_ref.shape[0]):
        away = ids_buf[k : k + 1, :] ^ me
        turned = (away & CORE) | ((away & XBIT) << 1) | ((away & YBIT) >> 1)
        away = jnp.where(me & CORE == 0, away, turned)
        route += jnp.where(row == away, gates[k : k + 1, :], 0.0)
    route = route.astype(jnp.bfloat16)
    for out_ref in out_refs:
        out_ref[out_ref.shape[0] - WEIGHT_ROWS :] = route
    for out_ref, part, copy in zip(out_refs, parts, copies[2:]):
        size = part.stop - part.start
        copy.wait()
        for k in range(width // LANES):
            out_ref[k * size : (k + 1) * size] = buf[part, k * LANES : (k + 1) * LANES]


def label(tokens, expert_ids, gate_weights):
    rows, width = tokens.shape
    parts = parts_of(rows)
    arrays = (tokens, expert_ids.T, gate_weights.T)
    lengths = [(p.stop - p.start) * width // LANES + WEIGHT_ROWS for p in parts]
    return pl.pallas_call(
        label_body,
        out_shape=[vmem_out((length, LANES)) for length in lengths],
        in_specs=[ANY_SPEC] * 3,
        out_specs=[VMEM_SPEC] * len(parts),
        scratch_shapes=[pltpu.VMEM(a.shape, a.dtype) for a in arrays]
        + [pltpu.SemaphoreType.DMA((2 + len(parts),))],
        compiler_params=pltpu.CompilerParams(vmem_limit_bytes=8 * MIB),
    )(*[pltpu.with_memory_space_constraint(a, pltpu.HBM) for a in arrays])


def after(value, *arrived):
    return lax.optimization_barrier((value, *arrived))[0]


def finish_body(*refs):
    terms, out_ref, (buf, sem) = refs[:-3], refs[-3], refs[-2:]
    rows = out_ref.shape[0] // PARTS
    copies = []
    for k in range(PARTS):
        part = slice(k * rows, (k + 1) * rows)
        buf[part] = sum(t[part].astype(jnp.float32) for t in terms).astype(jnp.bfloat16)
        at = pl.ds(k * rows, rows)
        copies.append(pltpu.make_async_copy(buf.at[at], out_ref.at[at], sem.at[k]))
        copies[-1].start()
    for copy in copies:
        copy.wait()


def finish(terms):
    shape = terms[0].shape
    return pl.pallas_call(
        finish_body,
        out_shape=jax.ShapeDtypeStruct(shape, jnp.bfloat16),
        in_specs=[VMEM_SPEC] * len(terms),
        out_specs=ANY_SPEC,
        scratch_shapes=[pltpu.VMEM(shape, jnp.bfloat16), pltpu.SemaphoreType.DMA((PARTS,))],
        compiler_params=pltpu.CompilerParams(vmem_limit_bytes=8 * MIB),
    )(*[in_vmem(a) for a in terms])


def stage_body(*refs):
    n = len(refs) // 2
    for src, dst in zip(refs[:n], refs[n:]):
        dst[...] = src[...]


def stage(parts, hint):
    n = len(parts)
    return pl.pallas_call(
        stage_body,
        out_shape=[vmem_out(p.shape) for p in parts],
        in_specs=[VMEM_SPEC] * n,
        out_specs=[VMEM_SPEC] * n,
        compiler_params=pltpu.CompilerParams(vmem_limit_bytes=8 * MIB),
        cost_estimate=pl.CostEstimate(
            flops=hint, bytes_accessed=4 * sum(p.size for p in parts), transcendentals=0
        ),
    )(*[in_vmem(p) for p in parts])


def add_body(a_ref, b_ref, out_ref):
    out_ref[...] = a_ref[...].astype(jnp.float32) + b_ref[...].astype(jnp.float32)


def add(a, b):
    return pl.pallas_call(
        add_body,
        out_shape=pltpu.VMEM(a.shape, jnp.float32),
        in_specs=[VMEM_SPEC] * 2,
        out_specs=VMEM_SPEC,
        compiler_params=pltpu.CompilerParams(vmem_limit_bytes=8 * MIB),
        cost_estimate=pl.CostEstimate(flops=10000000000, bytes_accessed=8 * a.size, transcendentals=0),
    )(in_vmem(a), in_vmem(b))


def fetch_body(n, blocks, *refs):
    arrays, parts, outs, whole, sem = refs[:n], refs[n:-n - 2], refs[-n - 2 : -2], refs[-2], refs[-1]
    copies = [pltpu.make_async_copy(arrays[k], outs[k], sem.at[k]) for k in range(n)]
    for copy in copies:
        copy.start()
    sizes = [(part.shape[0] - WEIGHT_ROWS) // blocks for part in parts]
    for k in range(blocks):
        at = k * sum(sizes)
        for part, size in zip(parts, sizes):
            whole[at : at + size] = part[k * size : (k + 1) * size]
            at += size
    whole[blocks * sum(sizes) :] = parts[0][blocks * sizes[0] :]
    for copy in copies:
        copy.wait()


def fetch(arrays, parts, width):
    n = len(arrays)
    length = sum(part.shape[0] - WEIGHT_ROWS for part in parts) + WEIGHT_ROWS
    return pl.pallas_call(
        functools.partial(fetch_body, n, width // LANES),
        out_shape=[vmem_out(a.shape) for a in arrays] + [vmem_out((length, LANES))],
        in_specs=[ANY_SPEC] * n + [VMEM_SPEC] * len(parts),
        out_specs=[VMEM_SPEC] * (n + 1),
        scratch_shapes=[pltpu.SemaphoreType.DMA((n,))],
        compiler_params=pltpu.CompilerParams(vmem_limit_bytes=8 * MIB),
        cost_estimate=pl.CostEstimate(
            flops=0, bytes_accessed=4 * sum(a.size for a in arrays), transcendentals=0
        ),
    )(
        *[pltpu.with_memory_space_constraint(a, pltpu.HBM) for a in arrays],
        *[in_vmem(part) for part in parts],
    )


def ffn_body(steps, n, *refs):
    x_refs, weights, (o_ref, x_buf, h_buf) = refs[:n], refs[n : n + 6], refs[n + 6 :]
    width, hidden = o_ref.shape[1], h_buf.shape[1] // 2
    parts = []
    for x_ref in x_refs:
        rows = (x_ref.shape[0] - WEIGHT_ROWS) * LANES // width
        blocks = [x_ref[k * rows : (k + 1) * rows] for k in range(width // LANES)]
        parts.append(jnp.concatenate(blocks, axis=1))
    x_buf[...] = jnp.concatenate(parts)
    route = x_refs[0][x_refs[0].shape[0] - WEIGHT_ROWS :].astype(jnp.float32)
    columns = []
    for row in (steps, steps ^ CORE):
        spread = jnp.broadcast_to(route[row : row + 1], (route.shape[1], route.shape[1]))
        columns.append(spread.T[:, :1])
    for e in range(2):
        w_gate, w_up = weights[3 * e], weights[3 * e + 1]
        for f in range(0, hidden, 256):
            x = x_buf[...]
            gate = jnp.dot(x, w_gate[:, f : f + 256], preferred_element_type=jnp.float32)
            up = jnp.dot(x, w_up[:, f : f + 256], preferred_element_type=jnp.float32)
            act = (gate / (1.0 + jnp.exp(-gate)) * up).astype(jnp.bfloat16)
            h_buf[:, e * hidden + f : e * hidden + f + 256] = act
    for c in range(0, width, 1024):
        out = None
        for e in range(2):
            act = h_buf[:, e * hidden : (e + 1) * hidden]
            part = jnp.dot(act, weights[3 * e + 2][:, c : c + 1024], preferred_element_type=jnp.float32)
            part = columns[e] * part
            out = part if out is None else out + part
        o_ref[:, c : c + 1024] = out.astype(jnp.bfloat16)


def ffn(blocks, steps, *, width, weights):
    hidden = weights[0].shape[1]
    rows = sum(block.shape[0] - WEIGHT_ROWS for block in blocks) * LANES // width
    return pl.pallas_call(
        functools.partial(ffn_body, steps, len(blocks)),
        out_shape=vmem_out((rows, width)),
        in_specs=[VMEM_SPEC] * (len(blocks) + 6),
        out_specs=VMEM_SPEC,
        scratch_shapes=[
            pltpu.VMEM((rows, width), jnp.bfloat16),
            pltpu.VMEM((rows, 2 * hidden), jnp.bfloat16),
        ],
        compiler_params=pltpu.CompilerParams(vmem_limit_bytes=16 * MIB),
        cost_estimate=pl.CostEstimate(
            flops=12 * rows * width * hidden,
            bytes_accessed=2 * sum(w.size for w in weights) + 4 * rows * width,
            transcendentals=2 * rows * hidden,
        ),
    )(*[in_vmem(a) for a in (*blocks, *weights)])


def two_by_two(tokens, expert_ids, gate_weights, w_gate, w_up, w_down):
    width = tokens.shape[1]
    halves = label(tokens, expert_ids, gate_weights)

    near = [hop(half, FIRST) for half in halves]
    own = (w_gate[0], w_up[0], w_down[0])
    *fetched, home = fetch(own, halves, width)
    swapped = [hop(w, CORE) for w in own]
    near = [after(half, fetched[0]) for half in near]
    far = stage([hop(half, SECOND) for half in near], 28000000000)
    side = [hop(after(home, *near, swapped[0]), SECOND)]

    run = functools.partial(ffn, width=width, weights=[*fetched, *swapped])
    far_out = run(far, FIRST | SECOND)
    passed = hop(far_out, FIRST)
    near_out = run([after(near[0], far_out), near[1]], FIRST)
    from_near = hop(near_out, FIRST)
    side_out = run([after(side[0], near_out), *side[1:]], SECOND)
    joined = side_out.astype(jnp.float32) + passed.astype(jnp.float32)
    joined = joined.astype(jnp.bfloat16)
    from_side = hop(joined, SECOND)
    home_out = run([after(home, joined)], 0)
    total = add(home_out, from_near)
    return finish([total, from_side])


def on_device(tokens, *rest):
    fits = lax.axis_size(AXIS) == 8 and tokens.shape[0] == LANES
    return (two_by_two if fits else any_slice)(tokens, *rest)


def solution(mesh):
    return jax.shard_map(
        on_device,
        mesh=mesh,
        in_specs=(
            P(("dp", AXIS), None),
            P(("dp", AXIS), None),
            P(("dp", AXIS), None),
            P(AXIS, None, None),
            P(AXIS, None, None),
            P(AXIS, None, None),
        ),
        out_specs=P(("dp", AXIS), None),
        check_vma=False,
    )
```

```python
import functools

import jax
import jax.numpy as jnp
from jax import lax
from jax.experimental import pallas as pl
from jax.experimental.pallas import tpu as pltpu
from jax.sharding import PartitionSpec as P

AXIS = "expert"
CORE, XBIT, YBIT = 1, 2, 4
FIRST, SECOND = 2, 4


def slot_table(routed, capacity):
    counted = routed.astype(jnp.int32)
    position = jnp.cumsum(counted, axis=1) - 1
    slot_ids = jnp.arange(capacity, dtype=jnp.int32)
    chosen = routed[:, None, :] & (position[:, None, :] == slot_ids[None, :, None])
    row_ids = jnp.arange(routed.shape[1], dtype=jnp.int32)
    slot_index = jnp.sum(jnp.where(chosen, row_ids[None, None, :], 0), axis=2)
    filled = jnp.any(chosen, axis=2)
    return (slot_index, filled)


def expert_ffn(slot_block, w_gate, w_up, w_down):
    width = slot_block.shape[-1]
    flat_rows = slot_block.reshape(-1, width)
    gate_act = jnp.dot(flat_rows, w_gate[0], preferred_element_type=jnp.float32)
    up_act = jnp.dot(flat_rows, w_up[0], preferred_element_type=jnp.float32)
    hidden = (jax.nn.silu(gate_act) * up_act).astype(jnp.bfloat16)
    expert_out = jnp.dot(hidden, w_down[0], preferred_element_type=jnp.float32)
    return expert_out.reshape(slot_block.shape[:-1] + (w_down.shape[2],))


def swap_all(rows):
    return lax.all_to_all(rows, AXIS, split_axis=0, concat_axis=0, tiled=True)


def route_table(expert_ids, gate_weights, experts):
    labels = jnp.arange(experts, dtype=jnp.int32)
    matched = expert_ids[:, :, None] == labels[None, None, :]
    weights = gate_weights.astype(jnp.float32)[:, :, None]
    return jnp.sum(jnp.where(matched, weights, jnp.float32(0.0)), axis=1)


def any_slice(tokens, expert_ids, gate_weights, w_gate, w_up, w_down):
    tok_dev, choose_k = expert_ids.shape
    width = tokens.shape[1]
    experts = w_gate.shape[0] * lax.axis_size(AXIS)
    capacity = min(tok_dev, 3 * tok_dev * choose_k // (2 * experts))
    weight = route_table(expert_ids, gate_weights, experts)
    home_index, home_filled = slot_table(weight.T != 0.0, capacity)
    arrived = swap_all(tokens[home_index])
    returned_rows = swap_all(expert_ffn(arrived, w_gate, w_up, w_down))
    owners = jnp.arange(experts, dtype=jnp.int32)[:, None]
    factor = jnp.where(home_filled, weight.T[owners, home_index], jnp.float32(0.0))
    combined = jnp.zeros((tok_dev, width), jnp.float32)
    combined = combined.at[home_index.reshape(-1)].add(
        (factor[:, :, None] * returned_rows).reshape(-1, width)
    )
    return combined.astype(jnp.bfloat16)


def hop(block, way):
    bits = {CORE: (CORE, CORE), FIRST: (YBIT, XBIT), SECOND: (XBIT, YBIT)}[way]
    pairs = [(i, i ^ bits[i & CORE]) for i in range(lax.axis_size(AXIS))]
    return lax.ppermute(block, AXIS, pairs)


def in_vmem(array):
    return pltpu.with_memory_space_constraint(array, pltpu.VMEM)


def vmem_out(shape):
    return pltpu.VMEM(shape, jnp.bfloat16)


MIB = 1 << 20
PARTS = 4
LANES = 128
WEIGHT_ROWS = 16
VMEM_SPEC = pl.BlockSpec(memory_space=pltpu.VMEM)
ANY_SPEC = pl.BlockSpec(memory_space=pl.ANY)


def parts_of(rows):
    return slice(0, rows // 2), slice(rows // 2, rows)


def label_body(tokens_ref, ids_ref, gates_ref, *refs):
    *out_refs, buf, ids_buf, gates_buf, sem = refs
    rows, width = buf.shape
    parts = parts_of(rows)
    pairs = [(ids_ref, ids_buf), (gates_ref, gates_buf)]
    for part in parts:
        at = pl.ds(part.start, part.stop - part.start)
        pairs.append((tokens_ref.at[at], buf.at[at]))
    copies = [pltpu.make_async_copy(src, dst, sem.at[k]) for k, (src, dst) in enumerate(pairs)]
    for copy in copies:
        copy.start()
    for copy in copies[:2]:
        copy.wait()
    me = lax.axis_index(AXIS)
    row = lax.broadcasted_iota(jnp.int32, (WEIGHT_ROWS, rows), 0)
    gates = gates_buf[...].astype(jnp.float32)
    route = jnp.zeros((WEIGHT_ROWS, rows), jnp.float32)
    for k in range(ids_ref.shape[0]):
        away = ids_buf[k : k + 1, :] ^ me
        turned = (away & CORE) | ((away & XBIT) << 1) | ((away & YBIT) >> 1)
        away = jnp.where(me & CORE == 0, turned, away)
        route += jnp.where(row == away, gates[k : k + 1, :], 0.0)
    route = route.astype(jnp.bfloat16)
    for out_ref in out_refs:
        out_ref[out_ref.shape[0] - WEIGHT_ROWS :] = route
    for out_ref, part, copy in zip(out_refs, parts, copies[2:]):
        size = part.stop - part.start
        copy.wait()
        for k in range(width // LANES):
            out_ref[k * size : (k + 1) * size] = buf[part, k * LANES : (k + 1) * LANES]


def label(tokens, expert_ids, gate_weights):
    rows, width = tokens.shape
    parts = parts_of(rows)
    arrays = (tokens, expert_ids.T, gate_weights.T)
    lengths = [(p.stop - p.start) * width // LANES + WEIGHT_ROWS for p in parts]
    return pl.pallas_call(
        label_body,
        out_shape=[vmem_out((length, LANES)) for length in lengths],
        in_specs=[ANY_SPEC] * 3,
        out_specs=[VMEM_SPEC] * len(parts),
        scratch_shapes=[pltpu.VMEM(a.shape, a.dtype) for a in arrays]
        + [pltpu.SemaphoreType.DMA((2 + len(parts),))],
        compiler_params=pltpu.CompilerParams(vmem_limit_bytes=8 * MIB),
    )(*[pltpu.with_memory_space_constraint(a, pltpu.HBM) for a in arrays])


def after(value, *arrived):
    return lax.optimization_barrier((value, *arrived))[0]


def finish_body(*refs):
    terms, out_ref, (buf, sem) = refs[:-3], refs[-3], refs[-2:]
    rows = out_ref.shape[0] // PARTS
    copies = []
    for k in range(PARTS):
        part = slice(k * rows, (k + 1) * rows)
        buf[part] = sum(t[part].astype(jnp.float32) for t in terms).astype(jnp.bfloat16)
        at = pl.ds(k * rows, rows)
        copies.append(pltpu.make_async_copy(buf.at[at], out_ref.at[at], sem.at[k]))
        copies[-1].start()
    for copy in copies:
        copy.wait()


def finish(terms):
    shape = terms[0].shape
    return pl.pallas_call(
        finish_body,
        out_shape=jax.ShapeDtypeStruct(shape, jnp.bfloat16),
        in_specs=[VMEM_SPEC] * len(terms),
        out_specs=ANY_SPEC,
        scratch_shapes=[pltpu.VMEM(shape, jnp.bfloat16), pltpu.SemaphoreType.DMA((PARTS,))],
        compiler_params=pltpu.CompilerParams(vmem_limit_bytes=8 * MIB),
    )(*[in_vmem(a) for a in terms])


def stage_body(*refs):
    n = len(refs) // 2
    for src, dst in zip(refs[:n], refs[n:]):
        dst[...] = src[...]


def stage(parts, hint):
    n = len(parts)
    return pl.pallas_call(
        stage_body,
        out_shape=[vmem_out(p.shape) for p in parts],
        in_specs=[VMEM_SPEC] * n,
        out_specs=[VMEM_SPEC] * n,
        compiler_params=pltpu.CompilerParams(vmem_limit_bytes=8 * MIB),
        cost_estimate=pl.CostEstimate(
            flops=hint, bytes_accessed=4 * sum(p.size for p in parts), transcendentals=0
        ),
    )(*[in_vmem(p) for p in parts])


def add_body(a_ref, b_ref, out_ref):
    out_ref[...] = a_ref[...].astype(jnp.float32) + b_ref[...].astype(jnp.float32)


def add(a, b):
    return pl.pallas_call(
        add_body,
        out_shape=pltpu.VMEM(a.shape, jnp.float32),
        in_specs=[VMEM_SPEC] * 2,
        out_specs=VMEM_SPEC,
        compiler_params=pltpu.CompilerParams(vmem_limit_bytes=8 * MIB),
        cost_estimate=pl.CostEstimate(flops=10000000000, bytes_accessed=8 * a.size, transcendentals=0),
    )(in_vmem(a), in_vmem(b))


def fetch_body(n, blocks, *refs):
    arrays, parts, outs, whole, sem = refs[:n], refs[n:-n - 2], refs[-n - 2 : -2], refs[-2], refs[-1]
    copies = [pltpu.make_async_copy(arrays[k], outs[k], sem.at[k]) for k in range(n)]
    for copy in copies:
        copy.start()
    sizes = [(part.shape[0] - WEIGHT_ROWS) // blocks for part in parts]
    for k in range(blocks):
        at = k * sum(sizes)
        for part, size in zip(parts, sizes):
            whole[at : at + size] = part[k * size : (k + 1) * size]
            at += size
    whole[blocks * sum(sizes) :] = parts[0][blocks * sizes[0] :]
    for copy in copies:
        copy.wait()


def fetch(arrays, parts, width):
    n = len(arrays)
    length = sum(part.shape[0] - WEIGHT_ROWS for part in parts) + WEIGHT_ROWS
    return pl.pallas_call(
        functools.partial(fetch_body, n, width // LANES),
        out_shape=[vmem_out(a.shape) for a in arrays] + [vmem_out((length, LANES))],
        in_specs=[ANY_SPEC] * n + [VMEM_SPEC] * len(parts),
        out_specs=[VMEM_SPEC] * (n + 1),
        scratch_shapes=[pltpu.SemaphoreType.DMA((n,))],
        compiler_params=pltpu.CompilerParams(vmem_limit_bytes=8 * MIB),
        cost_estimate=pl.CostEstimate(
            flops=0, bytes_accessed=4 * sum(a.size for a in arrays), transcendentals=0
        ),
    )(
        *[pltpu.with_memory_space_constraint(a, pltpu.HBM) for a in arrays],
        *[in_vmem(part) for part in parts],
    )


def ffn_body(steps, n, *refs):
    x_refs, weights, (o_ref, x_buf, h_buf) = refs[:n], refs[n : n + 6], refs[n + 6 :]
    width, hidden = o_ref.shape[1], h_buf.shape[1] // 2
    parts = []
    for x_ref in x_refs:
        rows = (x_ref.shape[0] - WEIGHT_ROWS) * LANES // width
        blocks = [x_ref[k * rows : (k + 1) * rows] for k in range(width // LANES)]
        parts.append(jnp.concatenate(blocks, axis=1))
    x_buf[...] = jnp.concatenate(parts)
    route = x_refs[0][x_refs[0].shape[0] - WEIGHT_ROWS :].astype(jnp.float32)
    columns = []
    for row in (steps, steps ^ CORE):
        spread = jnp.broadcast_to(route[row : row + 1], (route.shape[1], route.shape[1]))
        columns.append(spread.T[:, :1])
    for e in range(2):
        w_gate, w_up = weights[3 * e], weights[3 * e + 1]
        for f in range(0, hidden, 256):
            x = x_buf[...]
            gate = jnp.dot(x, w_gate[:, f : f + 256], preferred_element_type=jnp.float32)
            up = jnp.dot(x, w_up[:, f : f + 256], preferred_element_type=jnp.float32)
            act = (gate / (1.0 + jnp.exp(-gate)) * up).astype(jnp.bfloat16)
            h_buf[:, e * hidden + f : e * hidden + f + 256] = act
    for c in range(0, width, 1024):
        out = None
        for e in range(2):
            act = h_buf[:, e * hidden : (e + 1) * hidden]
            part = jnp.dot(act, weights[3 * e + 2][:, c : c + 1024], preferred_element_type=jnp.float32)
            part = columns[e] * part
            out = part if out is None else out + part
        o_ref[:, c : c + 1024] = out.astype(jnp.bfloat16)


def ffn(blocks, steps, *, width, weights):
    hidden = weights[0].shape[1]
    rows = sum(block.shape[0] - WEIGHT_ROWS for block in blocks) * LANES // width
    return pl.pallas_call(
        functools.partial(ffn_body, steps, len(blocks)),
        out_shape=vmem_out((rows, width)),
        in_specs=[VMEM_SPEC] * (len(blocks) + 6),
        out_specs=VMEM_SPEC,
        scratch_shapes=[
            pltpu.VMEM((rows, width), jnp.bfloat16),
            pltpu.VMEM((rows, 2 * hidden), jnp.bfloat16),
        ],
        compiler_params=pltpu.CompilerParams(vmem_limit_bytes=16 * MIB),
        cost_estimate=pl.CostEstimate(
            flops=12 * rows * width * hidden,
            bytes_accessed=2 * sum(w.size for w in weights) + 4 * rows * width,
            transcendentals=2 * rows * hidden,
        ),
    )(*[in_vmem(a) for a in (*blocks, *weights)])


def two_by_two(tokens, expert_ids, gate_weights, w_gate, w_up, w_down):
    width = tokens.shape[1]
    halves = label(tokens, expert_ids, gate_weights)

    near = [hop(half, FIRST) for half in halves]
    own = (w_gate[0], w_up[0], w_down[0])
    *fetched, home = fetch(own, halves, width)
    swapped = [hop(w, CORE) for w in own]
    near = [after(half, fetched[0]) for half in near]
    far = stage([hop(half, SECOND) for half in near], 28000000000)
    side = [hop(after(home, *near, swapped[0]), SECOND)]

    run = functools.partial(ffn, width=width, weights=[*fetched, *swapped])
    far_out = run(far, FIRST | SECOND)
    passed = hop(far_out, FIRST)
    near_out = run([after(near[0], far_out), near[1]], FIRST)
    from_near = hop(near_out, FIRST)
    side_out = run([after(side[0], near_out), *side[1:]], SECOND)
    joined = side_out.astype(jnp.float32) + passed.astype(jnp.float32)
    joined = joined.astype(jnp.bfloat16)
    from_side = hop(joined, SECOND)
    home_out = run([after(home, joined)], 0)
    total = add(home_out, from_near)
    return finish([total, from_side])


def on_device(tokens, *rest):
    fits = lax.axis_size(AXIS) == 8 and tokens.shape[0] == LANES
    return (two_by_two if fits else any_slice)(tokens, *rest)


def solution(mesh):
    return jax.shard_map(
        on_device,
        mesh=mesh,
        in_specs=(
            P(("dp", AXIS), None),
            P(("dp", AXIS), None),
            P(("dp", AXIS), None),
            P(AXIS, None, None),
            P(AXIS, None, None),
            P(AXIS, None, None),
        ),
        out_specs=P(("dp", AXIS), None),
        check_vma=False,
    )
```

```python
import functools

import jax
import jax.numpy as jnp
from jax import lax
from jax.experimental import pallas as pl
from jax.experimental.pallas import tpu as pltpu
from jax.sharding import PartitionSpec as P

AXIS = "expert"
CORE, XBIT, YBIT = 1, 2, 4
FIRST, SECOND = 2, 4


def slot_table(routed, capacity):
    counted = routed.astype(jnp.int32)
    position = jnp.cumsum(counted, axis=1) - 1
    slot_ids = jnp.arange(capacity, dtype=jnp.int32)
    chosen = routed[:, None, :] & (position[:, None, :] == slot_ids[None, :, None])
    row_ids = jnp.arange(routed.shape[1], dtype=jnp.int32)
    slot_index = jnp.sum(jnp.where(chosen, row_ids[None, None, :], 0), axis=2)
    filled = jnp.any(chosen, axis=2)
    return (slot_index, filled)


def expert_ffn(slot_block, w_gate, w_up, w_down):
    width = slot_block.shape[-1]
    flat_rows = slot_block.reshape(-1, width)
    gate_act = jnp.dot(flat_rows, w_gate[0], preferred_element_type=jnp.float32)
    up_act = jnp.dot(flat_rows, w_up[0], preferred_element_type=jnp.float32)
    hidden = (jax.nn.silu(gate_act) * up_act).astype(jnp.bfloat16)
    expert_out = jnp.dot(hidden, w_down[0], preferred_element_type=jnp.float32)
    return expert_out.reshape(slot_block.shape[:-1] + (w_down.shape[2],))


def swap_all(rows):
    return lax.all_to_all(rows, AXIS, split_axis=0, concat_axis=0, tiled=True)


def route_table(expert_ids, gate_weights, experts):
    labels = jnp.arange(experts, dtype=jnp.int32)
    matched = expert_ids[:, :, None] == labels[None, None, :]
    weights = gate_weights.astype(jnp.float32)[:, :, None]
    return jnp.sum(jnp.where(matched, weights, jnp.float32(0.0)), axis=1)


def any_slice(tokens, expert_ids, gate_weights, w_gate, w_up, w_down):
    tok_dev, choose_k = expert_ids.shape
    width = tokens.shape[1]
    experts = w_gate.shape[0] * lax.axis_size(AXIS)
    capacity = min(tok_dev, 3 * tok_dev * choose_k // (2 * experts))
    weight = route_table(expert_ids, gate_weights, experts)
    home_index, home_filled = slot_table(weight.T != 0.0, capacity)
    arrived = swap_all(tokens[home_index])
    returned_rows = swap_all(expert_ffn(arrived, w_gate, w_up, w_down))
    owners = jnp.arange(experts, dtype=jnp.int32)[:, None]
    factor = jnp.where(home_filled, weight.T[owners, home_index], jnp.float32(0.0))
    combined = jnp.zeros((tok_dev, width), jnp.float32)
    combined = combined.at[home_index.reshape(-1)].add(
        (factor[:, :, None] * returned_rows).reshape(-1, width)
    )
    return combined.astype(jnp.bfloat16)


def hop(block, way):
    bits = {CORE: (CORE, CORE), FIRST: (YBIT, XBIT), SECOND: (XBIT, YBIT)}[way]
    pairs = [(i, i ^ bits[i & CORE]) for i in range(lax.axis_size(AXIS))]
    return lax.ppermute(block, AXIS, pairs)


def in_vmem(array):
    return pltpu.with_memory_space_constraint(array, pltpu.VMEM)


def vmem_out(shape):
    return pltpu.VMEM(shape, jnp.bfloat16)


MIB = 1 << 20
PARTS = 2
LANES = 128
WEIGHT_ROWS = 16
VMEM_SPEC = pl.BlockSpec(memory_space=pltpu.VMEM)
ANY_SPEC = pl.BlockSpec(memory_space=pl.ANY)


def parts_of(rows):
    return slice(0, rows // 2), slice(rows // 2, rows)


def label_body(tokens_ref, ids_ref, gates_ref, *refs):
    *out_refs, buf, ids_buf, gates_buf, sem = refs
    rows, width = buf.shape
    parts = parts_of(rows)
    pairs = [(ids_ref, ids_buf), (gates_ref, gates_buf)]
    for part in parts:
        at = pl.ds(part.start, part.stop - part.start)
        pairs.append((tokens_ref.at[at], buf.at[at]))
    copies = [pltpu.make_async_copy(src, dst, sem.at[k]) for k, (src, dst) in enumerate(pairs)]
    for copy in copies:
        copy.start()
    for copy in copies[:2]:
        copy.wait()
    me = lax.axis_index(AXIS)
    row = lax.broadcasted_iota(jnp.int32, (WEIGHT_ROWS, rows), 0)
    gates = gates_buf[...].astype(jnp.float32)
    route = jnp.zeros((WEIGHT_ROWS, rows), jnp.float32)
    for k in range(ids_ref.shape[0]):
        away = ids_buf[k : k + 1, :] ^ me
        turned = (away & CORE) | ((away & XBIT) << 1) | ((away & YBIT) >> 1)
        away = jnp.where(me & CORE == 0, turned, away)
        route += jnp.where(row == away, gates[k : k + 1, :], 0.0)
    route = route.astype(jnp.bfloat16)
    for out_ref in out_refs:
        out_ref[out_ref.shape[0] - WEIGHT_ROWS :] = route
    for out_ref, part, copy in zip(out_refs, parts, copies[2:]):
        size = part.stop - part.start
        copy.wait()
        for k in range(width // LANES):
            out_ref[k * size : (k + 1) * size] = buf[part, k * LANES : (k + 1) * LANES]


def label(tokens, expert_ids, gate_weights):
    rows, width = tokens.shape
    parts = parts_of(rows)
    arrays = (tokens, expert_ids.T, gate_weights.T)
    lengths = [(p.stop - p.start) * width // LANES + WEIGHT_ROWS for p in parts]
    return pl.pallas_call(
        label_body,
        out_shape=[vmem_out((length, LANES)) for length in lengths],
        in_specs=[ANY_SPEC] * 3,
        out_specs=[VMEM_SPEC] * len(parts),
        scratch_shapes=[pltpu.VMEM(a.shape, a.dtype) for a in arrays]
        + [pltpu.SemaphoreType.DMA((2 + len(parts),))],
        compiler_params=pltpu.CompilerParams(vmem_limit_bytes=8 * MIB),
    )(*[pltpu.with_memory_space_constraint(a, pltpu.HBM) for a in arrays])


def after(value, *arrived):
    return lax.optimization_barrier((value, *arrived))[0]


def finish_body(*refs):
    terms, out_ref, (buf, sem) = refs[:-3], refs[-3], refs[-2:]
    rows = out_ref.shape[0] // PARTS
    copies = []
    for k in range(PARTS):
        part = slice(k * rows, (k + 1) * rows)
        buf[part] = sum(t[part].astype(jnp.float32) for t in terms).astype(jnp.bfloat16)
        at = pl.ds(k * rows, rows)
        copies.append(pltpu.make_async_copy(buf.at[at], out_ref.at[at], sem.at[k]))
        copies[-1].start()
    for copy in copies:
        copy.wait()


def finish(terms):
    shape = terms[0].shape
    return pl.pallas_call(
        finish_body,
        out_shape=jax.ShapeDtypeStruct(shape, jnp.bfloat16),
        in_specs=[VMEM_SPEC] * len(terms),
        out_specs=ANY_SPEC,
        scratch_shapes=[pltpu.VMEM(shape, jnp.bfloat16), pltpu.SemaphoreType.DMA((PARTS,))],
        compiler_params=pltpu.CompilerParams(vmem_limit_bytes=8 * MIB),
    )(*[in_vmem(a) for a in terms])


def stage_body(*refs):
    n = len(refs) // 2
    for src, dst in zip(refs[:n], refs[n:]):
        dst[...] = src[...]


def stage(parts, hint):
    n = len(parts)
    return pl.pallas_call(
        stage_body,
        out_shape=[vmem_out(p.shape) for p in parts],
        in_specs=[VMEM_SPEC] * n,
        out_specs=[VMEM_SPEC] * n,
        compiler_params=pltpu.CompilerParams(vmem_limit_bytes=8 * MIB),
        cost_estimate=pl.CostEstimate(
            flops=hint, bytes_accessed=4 * sum(p.size for p in parts), transcendentals=0
        ),
    )(*[in_vmem(p) for p in parts])


def add_body(a_ref, b_ref, out_ref):
    out_ref[...] = a_ref[...].astype(jnp.float32) + b_ref[...].astype(jnp.float32)


def add(a, b):
    return pl.pallas_call(
        add_body,
        out_shape=pltpu.VMEM(a.shape, jnp.float32),
        in_specs=[VMEM_SPEC] * 2,
        out_specs=VMEM_SPEC,
        compiler_params=pltpu.CompilerParams(vmem_limit_bytes=8 * MIB),
        cost_estimate=pl.CostEstimate(flops=10000000000, bytes_accessed=8 * a.size, transcendentals=0),
    )(in_vmem(a), in_vmem(b))


def fetch_body(n, blocks, *refs):
    arrays, parts, outs, whole, sem = refs[:n], refs[n:-n - 2], refs[-n - 2 : -2], refs[-2], refs[-1]
    copies = [pltpu.make_async_copy(arrays[k], outs[k], sem.at[k]) for k in range(n)]
    for copy in copies:
        copy.start()
    sizes = [(part.shape[0] - WEIGHT_ROWS) // blocks for part in parts]
    for k in range(blocks):
        at = k * sum(sizes)
        for part, size in zip(parts, sizes):
            whole[at : at + size] = part[k * size : (k + 1) * size]
            at += size
    whole[blocks * sum(sizes) :] = parts[0][blocks * sizes[0] :]
    for copy in copies:
        copy.wait()


def fetch(arrays, parts, width):
    n = len(arrays)
    length = sum(part.shape[0] - WEIGHT_ROWS for part in parts) + WEIGHT_ROWS
    return pl.pallas_call(
        functools.partial(fetch_body, n, width // LANES),
        out_shape=[vmem_out(a.shape) for a in arrays] + [vmem_out((length, LANES))],
        in_specs=[ANY_SPEC] * n + [VMEM_SPEC] * len(parts),
        out_specs=[VMEM_SPEC] * (n + 1),
        scratch_shapes=[pltpu.SemaphoreType.DMA((n,))],
        compiler_params=pltpu.CompilerParams(vmem_limit_bytes=8 * MIB),
        cost_estimate=pl.CostEstimate(
            flops=0, bytes_accessed=4 * sum(a.size for a in arrays), transcendentals=0
        ),
    )(
        *[pltpu.with_memory_space_constraint(a, pltpu.HBM) for a in arrays],
        *[in_vmem(part) for part in parts],
    )


def ffn_body(steps, n, *refs):
    x_refs, weights, (o_ref, x_buf, h_buf) = refs[:n], refs[n : n + 6], refs[n + 6 :]
    width, hidden = o_ref.shape[1], h_buf.shape[1] // 2
    parts = []
    for x_ref in x_refs:
        rows = (x_ref.shape[0] - WEIGHT_ROWS) * LANES // width
        blocks = [x_ref[k * rows : (k + 1) * rows] for k in range(width // LANES)]
        parts.append(jnp.concatenate(blocks, axis=1))
    x_buf[...] = jnp.concatenate(parts)
    route = x_refs[0][x_refs[0].shape[0] - WEIGHT_ROWS :].astype(jnp.float32)
    columns = []
    for row in (steps, steps ^ CORE):
        spread = jnp.broadcast_to(route[row : row + 1], (route.shape[1], route.shape[1]))
        columns.append(spread.T[:, :1])
    for e in range(2):
        w_gate, w_up = weights[3 * e], weights[3 * e + 1]
        for f in range(0, hidden, 256):
            x = x_buf[...]
            gate = jnp.dot(x, w_gate[:, f : f + 256], preferred_element_type=jnp.float32)
            up = jnp.dot(x, w_up[:, f : f + 256], preferred_element_type=jnp.float32)
            act = (gate / (1.0 + jnp.exp(-gate)) * up).astype(jnp.bfloat16)
            h_buf[:, e * hidden + f : e * hidden + f + 256] = act
    for c in range(0, width, 1024):
        out = None
        for e in range(2):
            act = h_buf[:, e * hidden : (e + 1) * hidden]
            part = jnp.dot(act, weights[3 * e + 2][:, c : c + 1024], preferred_element_type=jnp.float32)
            part = columns[e] * part
            out = part if out is None else out + part
        o_ref[:, c : c + 1024] = out.astype(jnp.bfloat16)


def ffn(blocks, steps, *, width, weights):
    hidden = weights[0].shape[1]
    rows = sum(block.shape[0] - WEIGHT_ROWS for block in blocks) * LANES // width
    return pl.pallas_call(
        functools.partial(ffn_body, steps, len(blocks)),
        out_shape=vmem_out((rows, width)),
        in_specs=[VMEM_SPEC] * (len(blocks) + 6),
        out_specs=VMEM_SPEC,
        scratch_shapes=[
            pltpu.VMEM((rows, width), jnp.bfloat16),
            pltpu.VMEM((rows, 2 * hidden), jnp.bfloat16),
        ],
        compiler_params=pltpu.CompilerParams(vmem_limit_bytes=16 * MIB),
        cost_estimate=pl.CostEstimate(
            flops=12 * rows * width * hidden,
            bytes_accessed=2 * sum(w.size for w in weights) + 4 * rows * width,
            transcendentals=2 * rows * hidden,
        ),
    )(*[in_vmem(a) for a in (*blocks, *weights)])


def two_by_two(tokens, expert_ids, gate_weights, w_gate, w_up, w_down):
    width = tokens.shape[1]
    halves = label(tokens, expert_ids, gate_weights)

    near = [hop(half, FIRST) for half in halves]
    own = (w_gate[0], w_up[0], w_down[0])
    *fetched, home = fetch(own, halves, width)
    swapped = [hop(w, CORE) for w in own]
    near[1] = after(near[1], fetched[0])
    far = stage([hop(half, SECOND) for half in near], 28000000000)
    side = [hop(after(home, *near, swapped[0]), SECOND)]

    run = functools.partial(ffn, width=width, weights=[*fetched, *swapped])
    far_out = run(far, FIRST | SECOND)
    passed = hop(far_out, FIRST)
    near_out = run([after(near[0], far_out), near[1]], FIRST)
    from_near = hop(near_out, FIRST)
    side_out = run([after(side[0], near_out), *side[1:]], SECOND)
    joined = side_out.astype(jnp.float32) + passed.astype(jnp.float32)
    joined = joined.astype(jnp.bfloat16)
    from_side = hop(joined, SECOND)
    home_out = run([after(home, joined)], 0)
    total = add(home_out, from_near)
    return finish([total, from_side])


def on_device(tokens, *rest):
    fits = lax.axis_size(AXIS) == 8 and tokens.shape[0] == LANES
    return (two_by_two if fits else any_slice)(tokens, *rest)


def solution(mesh):
    return jax.shard_map(
        on_device,
        mesh=mesh,
        in_specs=(
            P(("dp", AXIS), None),
            P(("dp", AXIS), None),
            P(("dp", AXIS), None),
            P(AXIS, None, None),
            P(AXIS, None, None),
            P(AXIS, None, None),
        ),
        out_specs=P(("dp", AXIS), None),
        check_vma=False,
    )
```
